256 devices in a mesh: row: 32 (over z, x), col: 8 (over y, core).
Axes of the slice: x: 4, y: 4, z: 8, core: 2. Of those that a mesh axis runs over, the one named last changes fastest.
Arguments:
- tiles: bfloat16 [32, 8, 64, 128, 128], P('row', 'col')
- block_rows: int32 [32, 8, 64], P('row', 'col'), may hold values from 0 to 15, as said below
- block_cols: int32 [32, 8, 64], P('row', 'col'), may hold values from 0 to 15, as said below
- tile_counts: int32 [32, 8], P('row', 'col'), may hold values from 16 to 64, as said below
- omega: bfloat16 [16384, 256], P('col'), may hold values from -6 to 6
Outputs:
- q_basis: bfloat16 [65536, 256], P('row')
- r_factor: float32 [256, 256], replicated
- z_sketch: float32 [16384, 256], P('col')
The draws below stay inside these ranges and needn't reach their ends.
Inputs may be any that keep to these rules, and one draw needn't show every extreme that they name: `block_rows`: on each device the first tile_counts slots name distinct tiles, i.e. distinct (row block, column block) pairs; a row block may appear in several slots; block rows lie below 16. `block_cols`: block columns lie below 16. `tile_counts`: some device uses all 64 slots.
All inputs are finite; a program needn't handle non-finite values.
Results may differ from the reference program's by a relative error of at most 0.015.
Values may be sent and summed in bfloat16 or wider, within the bound.
No kernel may reach another device: no remote copies, remote signals or barrier semaphores. Data moves between devices by JAX's collectives and lax.ppermute only.
A program may use at most 64 MiB of HBM per device.

```python
import math
import jax
import jax.numpy as jnp
from jax import lax

TILE = 128
K = 256
RB = 16
CB = 16
MAXT = 64
NROW = 65536
NCOL = 16384
N_ROW = 32
N_COL = 8


def slot_layout(key):
    keys = jax.random.split(key, N_ROW * N_COL)
    chosen = jax.vmap(lambda k: jax.random.permutation(k, RB * CB)[:MAXT])(keys)
    return chosen.reshape(N_ROW, N_COL, MAXT).astype(jnp.int32)


def draw_block_rows(key, part):
    return slot_layout(key) // CB


def draw_block_cols(key, part):
    return slot_layout(key) % CB


def draw_tile_counts(key, part):
    key = jax.random.fold_in(key, 11)
    first, second = jax.random.split(key)
    total = N_ROW * N_COL
    shifts = jax.random.randint(first, (total,), 0, 3)
    divisor = jnp.array([1, 2, 4], jnp.int32)[shifts]
    counts = MAXT // divisor
    fullest = jax.random.randint(second, (), 0, total)
    counts = jnp.where(jnp.arange(total) == fullest, MAXT, counts)
    return counts.reshape(N_ROW, N_COL).astype(jnp.int32)


def draw_tiles(key, part):
    key = jax.random.fold_in(key, 23)
    base_key, row_key, col_key = jax.random.split(key, 3)
    shape = (N_ROW, N_COL, MAXT, TILE, TILE)
    fan = 1.2 * NCOL * MAXT / (RB * CB)
    base = jax.random.exponential(base_key, shape, jnp.float32)
    span = math.log(10.0)
    norm = 2.0 * 4.6
    row_scale = jnp.exp(span * jax.random.uniform(row_key, (N_ROW, N_COL, MAXT, TILE, 1), jnp.float32))
    col_scale = jnp.exp(span * jax.random.uniform(col_key, (N_ROW, N_COL, MAXT, 1, TILE), jnp.float32))
    return (base * row_scale * col_scale / (norm * math.sqrt(fan))).astype(jnp.bfloat16)


def shard_levels(key, extent, shards, low, top_value):
    def one(position, blocks):
        draws = jax.random.uniform(jax.random.fold_in(jax.random.fold_in(key, 6), position), (blocks,), jnp.float32, low / len(shards), top_value / len(shards))
        return jnp.repeat(jnp.exp(draws), extent[position] // blocks).reshape((-1,) + (1,) * (len(extent) - position - 1))

    loudness = one(*shards[0])
    for cut in shards[1:]:
        loudness = loudness * one(*cut)
    return loudness


def centred(rng, shape, scale, limit, cuts=(), dtype=jnp.bfloat16):
    result = jax.random.normal(rng, shape, jnp.float32) * scale
    if len(cuts) > 0:
        result = shard_levels(rng, shape, cuts, -0.22, 0.18) * result
    return jnp.clip(result, min=-limit, max=limit).astype(dtype)


def setup_inputs(seed: int = 0) -> dict:
    seeds = jax.random.split(jax.random.key(seed), 6)
    return {
        "tiles": draw_tiles(jax.random.fold_in(seeds[5], 71), 0),
        "block_rows": draw_block_rows(jax.random.fold_in(seeds[5], 71), 0),
        "block_cols": draw_block_cols(jax.random.fold_in(seeds[5], 71), 0),
        "tile_counts": draw_tile_counts(jax.random.fold_in(seeds[5], 71), 0),
        "omega": centred(seeds[4], (NCOL, K), 1.0, 6.0, ((0, 8),)),
    }


def slab_sketch(tile_row, rows_row, cols_row, count_row, omega_blocks):
    ncol = tile_row.shape[0]
    slots = tile_row.shape[1]
    picked = omega_blocks[jnp.arange(ncol)[:, None], cols_row]
    prod = jnp.einsum('ctij,ctjk->ctik', tile_row.astype(jnp.float32), picked.astype(jnp.float32))
    mask = (jnp.arange(slots)[None, :] < count_row[:, None]).astype(jnp.float32)
    select = (rows_row[:, None, :] == jnp.arange(RB)[None, :, None]).astype(jnp.float32) * mask[:, None, :]
    return jnp.einsum('crt,ctik->rik', select, prod, precision=lax.Precision.HIGHEST)

def reference(tiles, block_rows, block_cols, tile_counts, omega):
    omega_blocks = omega.reshape(N_COL, CB, TILE, K)

    def one_slab(items):
        return slab_sketch(items[0], items[1], items[2], items[3], omega_blocks)
    sketch = lax.map(one_slab, (tiles, block_rows, block_cols, tile_counts)).reshape(NROW, K)
    gram = jnp.dot(sketch.T, sketch, precision=lax.Precision.HIGHEST) / NROW
    lower = jnp.linalg.cholesky(gram)
    q_basis = lax.linalg.triangular_solve(lower, sketch, left_side=False, lower=True, transpose_a=True).astype(jnp.bfloat16)
    q_blocks = q_basis.reshape(N_ROW, RB, TILE, K)

    def add_slab(total, items):
        tile_row, rows_row, cols_row, count_row, q_slab = items
        slots = tile_row.shape[1]
        picked = q_slab[rows_row]
        prod = jnp.einsum('ctij,ctik->ctjk', tile_row.astype(jnp.float32), picked.astype(jnp.float32))
        mask = (jnp.arange(slots)[None, :] < count_row[:, None]).astype(jnp.float32)
        select = (cols_row[:, None, :] == jnp.arange(CB)[None, :, None]).astype(jnp.float32) * mask[:, None, :]
        part = jnp.einsum('cbt,ctjk->cbjk', select, prod, precision=lax.Precision.HIGHEST)
        return (total + part.reshape(NCOL, K), None)
    start = jnp.zeros((NCOL, K), jnp.float32)
    z_sketch, unused = lax.scan(add_slab, start, (tiles, block_rows, block_cols, tile_counts, q_blocks))
    return (q_basis, lower.T, z_sketch)
```

```python
import jax
import jax.numpy as jnp
from jax import lax
from jax.experimental import pallas as pl
from jax.experimental.pallas import tpu as pltpu
from jax.sharding import Mesh, PartitionSpec as P

F32 = jnp.float32
BF16 = jnp.bfloat16
TILE = 128
K = 256
RB = 16
CB = 16
SLOTS = 64
HALF = RB * TILE // 2
NROW = 65536
PARTS = 32
ROWS = CB * TILE // PARTS
EXTRA = 16
GROUP = 4
NB = 32
VMEM = pl.BlockSpec(memory_space=pltpu.VMEM)
SMEM = pl.BlockSpec(memory_space=pltpu.SMEM)


def dot(a, b, ca, cb, precision=None):
    return lax.dot_general(
        a, b, (((ca,), (cb,)), ((), ())), precision=precision, preferred_element_type=F32
    )


def iota(shape, dim):
    return lax.broadcasted_iota(jnp.int32, shape, dim)


def sketch_kernel(core_ref, rows_ref, cols_ref, live_ref, tiles_ref, omega_ref, keep_ref, send_ref, acc):
    acc[...] = jnp.zeros_like(acc)
    live = live_ref[0]
    turn = core_ref[0] * (RB // 2)

    @pl.loop(0, (live + GROUP - 1) // GROUP)
    def _(g):
        prods, places = [], []
        for i in range(GROUP):
            t = g * GROUP + i
            prod = dot(tiles_ref[t], omega_ref[cols_ref[t] & (CB - 1)], 1, 0)
            prods.append(jnp.where(t < live, prod, 0.0))
            places.append((rows_ref[t] + turn) & (RB - 1))
        for prod, place in zip(prods, places):
            acc[place] += prod

    keep_ref[...] = acc[: RB // 2].reshape(HALF, K)
    send_ref[...] = acc[RB // 2 :].reshape(HALF, K)


def place_matrix(rows, cols, shift, dtype=BF16):
    e = iota((rows, cols), 0)
    p = iota((rows, cols), 1)
    return jnp.where((p // 6) * EXTRA + p % 6 + shift == e, 1.0, 0.0).astype(dtype)


def back_kernel(core_ref, rows_ref, cols_ref, live_ref, tiles_ref, mine_ref, other_ref, out_ref, s_ref, acc):
    core = core_ref[0]
    s_ref[pl.ds(core * (RB // 2), RB // 2)] = mine_ref[...].reshape(RB // 2, TILE, K)
    s_ref[pl.ds((1 - core) * (RB // 2), RB // 2)] = other_ref[...].reshape(RB // 2, TILE, K)
    acc[...] = jnp.zeros_like(acc)
    live = live_ref[0]

    @pl.loop(0, (live + GROUP - 1) // GROUP)
    def _(g):
        prods, places = [], []
        for i in range(GROUP):
            t = g * GROUP + i
            prod = dot(tiles_ref[t], s_ref[rows_ref[t] & (RB - 1)], 0, 0)
            prods.append(jnp.where(t < live, prod, 0.0))
            places.append(cols_ref[t] & (CB - 1))
        for prod, place in zip(prods, places):
            acc[place] += prod

    gram = dot(mine_ref[...], mine_ref[...], 0, 0) + dot(other_ref[...], other_ref[...], 0, 0)
    gram = gram * (1.0 / NROW)
    low = gram[K // 2 :, K // 2 :]
    low = jnp.concatenate([low[: K // 4], low[K // 4 :]], axis=1)
    packed = jnp.concatenate([gram[: K // 2], low], axis=0)
    high = packed.astype(BF16)
    rest = (packed - high.astype(F32)).astype(BF16)
    extra = dot(place_matrix(PARTS * EXTRA, 192, 0), high, 1, 0) + dot(
        place_matrix(PARTS * EXTRA, 192, 6), rest, 1, 0
    )
    out_ref[:, :ROWS, :] = acc[...].reshape(PARTS, ROWS, K).astype(BF16)
    out_ref[:, ROWS:, :] = extra.reshape(PARTS, EXTRA, K).astype(BF16)


def sum_kernel(in_ref, out_ref):
    total = in_ref[0].astype(F32)
    for i in range(1, PARTS):
        total = total + in_ref[i].astype(F32)
    w = total[:ROWS]
    extra = total[ROWS:]
    mean = jnp.sum(w, axis=0, keepdims=True) * (1.0 / ROWS)
    top = jnp.max(jnp.abs(mean), axis=1, keepdims=True)
    lead = (mean / jnp.maximum(top, 1e-30)).astype(BF16)
    leadf = lead.astype(F32)
    norm = jnp.maximum(jnp.sum(leadf * leadf, axis=1, keepdims=True), 0.5)
    coef = (dot(lead, w.astype(BF16), 1, 1) / norm).astype(BF16)
    rest = w - dot(coef, lead, 0, 0)
    row = iota((EXTRA, K), 0)
    gram = extra + pltpu.roll(extra, EXTRA - 6, 0)
    high = gram.astype(BF16).astype(F32)
    low = pltpu.roll(gram - high, 6, 0)
    wide = jnp.concatenate([coef.astype(F32), jnp.zeros((1, K - ROWS), F32)], axis=1)
    tail = jnp.where(row < 6, high, jnp.where(row < 12, low, 0.0))
    tail = jnp.where(row == 12, leadf, jnp.where(row == 13, wide, tail))
    body = rest.astype(BF16)
    tail = tail.astype(BF16)
    for i in range(PARTS):
        out_ref[i, :ROWS, :] = body
        out_ref[i, ROWS:, :] = tail


def factor(work):
    for b in range(K // NB):
        at = b * NB
        base = at // 128 * 128
        x = work[at : at + NB, base : base + 128]
        if at > base:
            x = pltpu.roll(x, 128 - (at - base), 1)
        lane = iota((NB, 128), 1)
        row = iota((NB, 128), 0)
        x = jnp.where(lane < NB, x, jnp.where(lane - NB == row, 1.0, 0.0))
        for j in range(NB):
            pivot = x[j : j + 1, :]
            scale = 1.0 / pivot[:, j : j + 1]
            m = jnp.where(row[:, :1] > j, x[:, j : j + 1] * scale, 0.0)
            x = x - m * pivot
        diag = jnp.sum(jnp.where(lane == row, x, 0.0), axis=1, keepdims=True)
        x = x * lax.rsqrt(diag)
        inv = pltpu.roll(x, 128 - NB, 1)[:, :NB]
        u = dot(inv, work[at : at + NB, :], 1, 0, lax.Precision.HIGHEST)
        work[at : at + NB, :] = u
        if at + NB < K:
            ut = u[:, :K].T
            work[at + NB :, :] -= dot(ut[at + NB :], u, 1, 0, lax.Precision.HIGHEST)


def final_kernel(core_ref, in_ref, mine_ref, other_ref, q_ref, r_ref, z_ref, work):
    extra = in_ref[:, ROWS:, :].reshape(PARTS * EXTRA, K)
    p = iota((192, PARTS * EXTRA), 0)
    e = iota((192, PARTS * EXTRA), 1)
    first = (p // 6) * EXTRA + p % 6
    pick = jnp.where((e == first) | (e == first + 6), 1.0, 0.0).astype(BF16)
    packed = dot(pick, extra, 1, 0)
    work[: K // 2, :K] = packed[: K // 2]
    work[K // 2 :, : K // 2] = packed[: K // 2, K // 2 :].T
    work[K // 2 : 3 * K // 4, K // 2 : K] = packed[K // 2 :, : K // 2]
    work[3 * K // 4 :, K // 2 : K] = packed[K // 2 :, K // 2 :]
    work[:, K:] = jnp.where(iota((K, K), 0) == iota((K, K), 1), 1.0, 0.0)
    factor(work)
    r_ref[...] = jnp.where(iota((K, K), 0) <= iota((K, K), 1), work[:, :K], 0.0)
    inv = work[:, K:]
    high = inv.astype(BF16)
    low = (inv - high.astype(F32)).astype(BF16)

    def solve(a):
        return dot(a, high, 1, 1) + dot(a, low, 1, 1)

    core = core_ref[0]
    q_ref[pl.ds(pl.multiple_of(core * HALF, HALF), HALF), :] = solve(mine_ref[...]).astype(BF16)
    q_ref[pl.ds(pl.multiple_of((1 - core) * HALF, HALF), HALF), :] = solve(other_ref[...]).astype(BF16)
    i = iota((2 * PARTS, PARTS * EXTRA), 0)
    e = iota((2 * PARTS, PARTS * EXTRA), 1)
    want = jnp.where(i < PARTS, i * EXTRA + 12, (i - PARTS) * EXTRA + 13)
    leads = dot(jnp.where(e == want, 1.0, 0.0).astype(BF16), extra, 1, 0)
    lead = solve(leads[:PARTS].astype(BF16))
    lead_high = lead.astype(BF16)
    lead_low = (lead - lead_high.astype(F32)).astype(BF16)
    coef = leads[PARTS:].astype(BF16)
    for i in range(PARTS):
        c = coef[i : i + 1, :ROWS]
        term = dot(c, lead_high[i : i + 1], 0, 0) + dot(c, lead_low[i : i + 1], 0, 0)
        z_ref[i * ROWS : (i + 1) * ROWS, :] = solve(in_ref[i, :ROWS, :]) + term


def shape(*dims, dtype=F32):
    return jax.ShapeDtypeStruct(dims, dtype)


LIMIT = pltpu.CompilerParams(vmem_limit_bytes=40 * 1024 * 1024)


def on_device(tiles, block_rows, block_cols, tile_counts, omega):
    core = lax.axis_index("c").astype(jnp.int32).reshape(1)
    rows = block_rows[0, 0]
    cols = block_cols[0, 0]
    live = tile_counts[0]
    tiles = tiles[0, 0]
    keep, send = pl.pallas_call(
        sketch_kernel,
        out_shape=(shape(HALF, K), shape(HALF, K)),
        in_specs=[SMEM] * 4 + [VMEM] * 2,
        out_specs=(VMEM, VMEM),
        scratch_shapes=[pltpu.VMEM((RB, TILE, K), F32)],
        compiler_params=LIMIT,
        name="sketch",
    )(core, rows, cols, live, tiles, omega.reshape(CB, TILE, K))
    swap = [(0, 1), (1, 0)]
    half = keep + lax.ppermute(send, "c", swap)
    quarters = lax.all_to_all(half.astype(BF16).reshape(4, HALF // 4, K), "y", 0, 0, tiled=True)
    shard = jnp.sum(quarters.astype(F32), axis=0).astype(BF16)
    spread = jnp.broadcast_to(shard[None], (4, HALF // 4, K))
    mine = lax.all_to_all(spread, "y", 0, 0, tiled=True).reshape(HALF, K)
    other = lax.ppermute(mine, "c", swap)
    payload = pl.pallas_call(
        back_kernel,
        out_shape=shape(PARTS, ROWS + EXTRA, K, dtype=BF16),
        in_specs=[SMEM] * 4 + [VMEM] * 3,
        out_specs=VMEM,
        scratch_shapes=[pltpu.VMEM((RB, TILE, K), BF16), pltpu.VMEM((CB, TILE, K), F32)],
        compiler_params=LIMIT,
        name="back",
    )(core, rows, cols, live, tiles, mine, other)
    parts = lax.all_to_all(payload, ("z", "x"), 0, 0, tiled=True)
    spread = pl.pallas_call(
        sum_kernel,
        out_shape=shape(PARTS, ROWS + EXTRA, K, dtype=BF16),
        in_specs=[VMEM],
        out_specs=VMEM,
        compiler_params=LIMIT,
        name="total",
    )(parts)
    whole = lax.all_to_all(spread, ("z", "x"), 0, 0, tiled=True)
    return pl.pallas_call(
        final_kernel,
        out_shape=(shape(2 * HALF, K, dtype=BF16), shape(K, K), shape(CB * TILE, K)),
        in_specs=[SMEM] + [VMEM] * 3,
        out_specs=(VMEM, VMEM, VMEM),
        scratch_shapes=[pltpu.VMEM((K, 2 * K), F32)],
        compiler_params=LIMIT,
        name="finish",
    )(core, whole, mine, other)


def solution(mesh):
    grid = Mesh(mesh.devices.reshape(8, 4, 4, 2), ("z", "x", "y", "c"))
    row, col = ("z", "x"), ("y", "c")
    placed = (
        P(row, col, None, None, None),
        P(row, col, None),
        P(row, col, None),
        P(row, col),
        P(col, None),
    )
    return jax.shard_map(
        on_device,
        mesh=grid,
        in_specs=placed,
        out_specs=(P(row, None), P(), P(col, None)),
        check_vma=False,
    )
```

```python
import jax
import jax.numpy as jnp
from jax import lax
from jax.experimental import pallas as pl
from jax.experimental.pallas import tpu as pltpu
from jax.sharding import Mesh, PartitionSpec as P

F32 = jnp.float32
BF16 = jnp.bfloat16
TILE = 128
K = 256
RB = 16
CB = 16
SLOTS = 64
HALF = RB * TILE // 2
NROW = 65536
PARTS = 32
ROWS = CB * TILE // PARTS
EXTRA = 16
GROUP = 4
NB = 64
LOAD = 8
PIECE = HALF // 4
VMEM = pl.BlockSpec(memory_space=pltpu.VMEM)
SMEM = pl.BlockSpec(memory_space=pltpu.SMEM)
HBM = pl.BlockSpec(memory_space=pltpu.HBM)


def dot(a, b, ca, cb, precision=None):
    return lax.dot_general(
        a, b, (((ca,), (cb,)), ((), ())), precision=precision, preferred_element_type=F32
    )


def iota(shape, dim):
    return lax.broadcasted_iota(jnp.int32, shape, dim)


def sketch_kernel(where_ref, rows_hbm, cols_hbm, live_hbm, tiles_hbm, omega_hbm, keep_ref, send_ref,
                  acc, rows_ref, cols_ref, live_ref, tiles_ref, omega_ref, small_sem, tile_sem):
    small = [
        pltpu.make_async_copy(rows_hbm, rows_ref, small_sem.at[0]),
        pltpu.make_async_copy(cols_hbm, cols_ref, small_sem.at[1]),
        pltpu.make_async_copy(live_hbm, live_ref, small_sem.at[2]),
        pltpu.make_async_copy(omega_hbm, omega_ref, small_sem.at[3]),
    ]
    big = [
        pltpu.make_async_copy(
            tiles_hbm.at[0, 0, pl.ds(g * LOAD, LOAD)], tiles_ref.at[pl.ds(g * LOAD, LOAD)], tile_sem.at[g]
        )
        for g in range(SLOTS // LOAD)
    ]
    for copy in small + big:
        copy.start()
    acc[...] = jnp.zeros_like(acc)
    for copy in small:
        copy.wait()
    live = live_ref[0, 0]
    core, chip = where_ref[0], where_ref[1]
    for g, copy in enumerate(big):
        copy.wait()

        @pl.when(g * LOAD < live)
        def _():
            prods, places = [], []
            for t in range(g * LOAD, (g + 1) * LOAD):
                prod = dot(tiles_ref[t], omega_ref[cols_ref[0, 0, t] & (CB - 1)], 1, 0)
                prods.append(jnp.where(t < live, prod, 0.0))
                block = rows_ref[0, 0, t] & (RB - 1)
                half = (block // 8 + core) & 1
                places.append(half * 8 + ((block - 2 * chip) & 7))
            for prod, place in zip(prods, places):
                acc[place] += prod

    keep_ref[...] = acc[: RB // 2].reshape(HALF, K)
    send_ref[...] = acc[RB // 2 :].reshape(HALF, K)


def place_matrix(rows, cols, shift, dtype=BF16):
    e = iota((rows, cols), 0)
    p = iota((rows, cols), 1)
    return jnp.where((p // 6) * EXTRA + p % 6 + shift == e, 1.0, 0.0).astype(dtype)


def back_kernel(where_ref, rows_ref, cols_ref, live_ref, tiles_ref, mine_ref, other_ref, out_ref, s_ref, acc):
    core, chip = where_ref[0], where_ref[1]
    for k in range(4):
        at = ((chip - k) & 3) * 2
        part = pl.ds(k * PIECE, PIECE)
        s_ref[pl.ds(core * 8 + at, 2)] = mine_ref[part, :].reshape(2, TILE, K)
        s_ref[pl.ds((1 - core) * 8 + at, 2)] = other_ref[part, :].reshape(2, TILE, K)
    acc[...] = jnp.zeros_like(acc)
    live = live_ref[0]

    @pl.loop(0, (live + GROUP - 1) // GROUP)
    def _(g):
        prods, places = [], []
        for i in range(GROUP):
            t = g * GROUP + i
            prod = dot(tiles_ref[t], s_ref[rows_ref[t] & (RB - 1)], 0, 0)
            prods.append(jnp.where(t < live, prod, 0.0))
            places.append(cols_ref[t] & (CB - 1))
        for prod, place in zip(prods, places):
            acc[place] += prod

    gram = dot(mine_ref[...], mine_ref[...], 0, 0) + dot(other_ref[...], other_ref[...], 0, 0)
    gram = gram * (1.0 / NROW)
    low = gram[K // 2 :, K // 2 :]
    low = jnp.concatenate([low[: K // 4], low[K // 4 :]], axis=1)
    packed = jnp.concatenate([gram[: K // 2], low], axis=0)
    high = packed.astype(BF16)
    rest = (packed - high.astype(F32)).astype(BF16)
    extra = dot(place_matrix(PARTS * EXTRA, 192, 0), high, 1, 0) + dot(
        place_matrix(PARTS * EXTRA, 192, 6), rest, 1, 0
    )
    out_ref[:, :ROWS, :] = acc[...].reshape(PARTS, ROWS, K).astype(BF16)
    out_ref[:, ROWS:, :] = extra.reshape(PARTS, EXTRA, K).astype(BF16)


def resplit(extra):
    row = iota(extra.shape, 0) % EXTRA
    gram = extra + pltpu.roll(extra, extra.shape[0] - 6, 0)
    high = gram.astype(BF16).astype(F32)
    low = pltpu.roll(gram - high, 6, 0)
    return jnp.where(row < 6, high, jnp.where(row < 12, low, 0.0))


def partial_kernel(in_ref, out_ref):
    total = in_ref[0].astype(F32)
    for i in range(1, 4):
        total = total + in_ref[i].astype(F32)
    out_ref[:, :ROWS, :] = total[:, :ROWS, :].astype(BF16)
    extra = resplit(total[:, ROWS:, :].reshape(8 * EXTRA, K))
    out_ref[:, ROWS:, :] = extra.reshape(8, EXTRA, K).astype(BF16)


def sum_kernel(in_ref, out_ref):
    total = in_ref[0].astype(F32)
    for i in range(1, 8):
        total = total + in_ref[i].astype(F32)
    w = total[:ROWS]
    mean = jnp.sum(w, axis=0, keepdims=True) * (1.0 / ROWS)
    top = jnp.max(jnp.abs(mean), axis=1, keepdims=True)
    lead = (mean / jnp.maximum(top, 1e-30)).astype(BF16)
    leadf = lead.astype(F32)
    norm = jnp.maximum(jnp.sum(leadf * leadf, axis=1, keepdims=True), 0.5)
    coef = (dot(lead, w.astype(BF16), 1, 1) / norm).astype(BF16)
    rest = w - dot(coef, lead, 0, 0)
    row = iota((EXTRA, K), 0)
    wide = jnp.concatenate([coef.astype(F32), jnp.zeros((1, K - ROWS), F32)], axis=1)
    tail = jnp.where(row == 12, leadf, jnp.where(row == 13, wide, resplit(total[ROWS:])))
    body = rest.astype(BF16)
    tail = tail.astype(BF16)
    for i in range(8):
        out_ref[i, :ROWS, :] = body
        out_ref[i, ROWS:, :] = tail


def eliminate(x):
    groups = NB // 8
    xs = [x[8 * g : 8 * g + 8] for g in range(groups)]
    sub = iota((8, 128), 0)

    def wide(a):
        return jnp.broadcast_to(a, (8, 128))

    for t in range(groups):
        at = 8 * t
        head = xs[t]
        cols = [wide(head[:, at + m : at + m + 1]) for m in range(8)]
        s = [[wide(cols[m][i : i + 1, :]) if m >= i else None for m in range(8)] for i in range(8)]
        rows = [wide(head[i : i + 1, :]) for i in range(8)]
        ratio = [[None] * 8 for _ in range(8)]
        scaled = []
        for j in range(8):
            inv = pltpu.reciprocal(s[j][j], approx=True)
            inv = inv * (2.0 - s[j][j] * inv)
            for m in range(j + 1, 8):
                ratio[j][m] = s[j][m] * inv
            for i in range(j + 1, 8):
                for m in range(i, 8):
                    s[i][m] = s[i][m] - ratio[j][i] * s[j][m]
                rows[i] = rows[i] - ratio[j][i] * rows[j]
            scaled.append(rows[j] * inv)
        for g in range(t + 1, groups):
            left, x = [], xs[g]
            for j in range(8):
                e = wide(xs[g][:, at + j : at + j + 1])
                for m in range(j):
                    e = e - ratio[m][j] * left[m]
                left.append(e)
                x = x - e * scaled[j]
            xs[g] = x
        out = rows[0] * lax.rsqrt(s[0][0])
        for j in range(1, 8):
            out = jnp.where(sub == j, rows[j] * lax.rsqrt(s[j][j]), out)
        xs[t] = out
    return jnp.concatenate(xs, axis=0)


def factor(work):
    lane = iota((NB, 128), 1)
    row = iota((NB, 128), 0)
    for b in range(K // NB):
        at = b * NB
        base = at // 128 * 128
        x = work[at : at + NB, base : base + 128]
        if at > base:
            x = pltpu.roll(x, 128 - (at - base), 1)
        x = eliminate(jnp.where(lane < NB, x, jnp.where(lane - NB == row, 1.0, 0.0)))
        inv = pltpu.roll(x, 128 - NB, 1)[:, :NB]
        u = dot(inv, work[at : at + NB, :], 1, 0, lax.Precision.HIGHEST)
        work[at : at + NB, :] = u
        if at + NB < K:
            ut = u[:, :K].T
            work[at + NB :, :] -= dot(ut[at + NB :], u, 1, 0, lax.Precision.HIGHEST)


def final_kernel(where_ref, in_ref, mine_ref, other_ref, q_ref, r_ref, z_ref, work):
    extra = in_ref[:, ROWS:, :].reshape(PARTS * EXTRA, K)
    p = iota((192, PARTS * EXTRA), 0)
    e = iota((192, PARTS * EXTRA), 1)
    first = (p // 6) * EXTRA + p % 6
    pick = jnp.where((e == first) | (e == first + 6), 1.0, 0.0).astype(BF16)
    packed = dot(pick, extra, 1, 0)
    work[: K // 2, :K] = packed[: K // 2]
    work[K // 2 :, : K // 2] = packed[: K // 2, K // 2 :].T
    work[K // 2 : 3 * K // 4, K // 2 : K] = packed[K // 2 :, : K // 2]
    work[3 * K // 4 :, K // 2 : K] = packed[K // 2 :, K // 2 :]
    work[:, K:] = jnp.where(iota((K, K), 0) == iota((K, K), 1), 1.0, 0.0)
    factor(work)
    r_ref[...] = jnp.where(iota((K, K), 0) <= iota((K, K), 1), work[:, :K], 0.0)
    inv = work[:, K:]
    high = inv.astype(BF16)
    low = (inv - high.astype(F32)).astype(BF16)

    def solve(a):
        return dot(a, high, 1, 1) + dot(a, low, 1, 1)

    core, chip = where_ref[0], where_ref[1]
    for half, ref in ((core, mine_ref), (1 - core, other_ref)):
        for k in range(4):
            at = pl.multiple_of(half * HALF + ((chip - k) & 3) * PIECE, PIECE)
            q_ref[pl.ds(at, PIECE), :] = solve(ref[k * PIECE : (k + 1) * PIECE, :]).astype(BF16)
    i = iota((2 * PARTS, PARTS * EXTRA), 0)
    e = iota((2 * PARTS, PARTS * EXTRA), 1)
    want = jnp.where(i < PARTS, i * EXTRA + 12, (i - PARTS) * EXTRA + 13)
    leads = dot(jnp.where(e == want, 1.0, 0.0).astype(BF16), extra, 1, 0)
    lead = solve(leads[:PARTS].astype(BF16))
    lead_high = lead.astype(BF16)
    lead_low = (lead - lead_high.astype(F32)).astype(BF16)
    coef = leads[PARTS:].astype(BF16)
    for i in range(PARTS):
        c = coef[i : i + 1, :ROWS]
        term = dot(c, lead_high[i : i + 1], 0, 0) + dot(c, lead_low[i : i + 1], 0, 0)
        z_ref[i * ROWS : (i + 1) * ROWS, :] = solve(in_ref[i, :ROWS, :]) + term


def shape(*dims, dtype=F32):
    return jax.ShapeDtypeStruct(dims, dtype)


LIMIT = pltpu.CompilerParams(vmem_limit_bytes=40 * 1024 * 1024)


def on_device(tiles, block_rows, block_cols, tile_counts, omega):
    where = jnp.stack([lax.axis_index("c"), lax.axis_index("y")]).astype(jnp.int32)
    swap = [(0, 1), (1, 0)]
    keep, send = pl.pallas_call(
        sketch_kernel,
        out_shape=(shape(HALF, K), shape(HALF, K)),
        in_specs=[SMEM] + [HBM] * 5,
        out_specs=(VMEM, VMEM),
        scratch_shapes=[
            pltpu.VMEM((RB, TILE, K), F32),
            pltpu.SMEM((1, 1, SLOTS), jnp.int32),
            pltpu.SMEM((1, 1, SLOTS), jnp.int32),
            pltpu.SMEM((1, 1), jnp.int32),
            pltpu.VMEM((SLOTS, TILE, TILE), BF16),
            pltpu.VMEM((CB, TILE, K), BF16),
            pltpu.SemaphoreType.DMA((4,)),
            pltpu.SemaphoreType.DMA((SLOTS // LOAD,)),
        ],
        compiler_params=LIMIT,
        name="sketch",
    )(where, block_rows, block_cols, tile_counts, tiles, omega.reshape(CB, TILE, K))

    def turn(a, k):
        return lax.ppermute(a, "y", [(i, (i + k) % 4) for i in range(4)])

    half = keep + lax.ppermute(send, "c", swap)
    quarters = half.reshape(4, PIECE, K)
    shard = quarters[0]
    for k in (2, 1, 3):
        shard = shard + turn(quarters[k].astype(BF16), k).astype(F32)
    shard = shard.astype(BF16)
    mine = jnp.concatenate([shard] + [turn(shard, k) for k in (1, 2, 3)], axis=0)
    other = lax.ppermute(mine, "c", swap)
    payload = pl.pallas_call(
        back_kernel,
        out_shape=shape(PARTS, ROWS + EXTRA, K, dtype=BF16),
        in_specs=[SMEM] * 4 + [VMEM] * 3,
        out_specs=VMEM,
        scratch_shapes=[pltpu.VMEM((RB, TILE, K), BF16), pltpu.VMEM((CB, TILE, K), F32)],
        compiler_params=LIMIT,
        name="back",
    )(where, block_rows[0, 0], block_cols[0, 0], tile_counts[0], tiles[0, 0], mine, other)
    size = (ROWS + EXTRA, K)
    parts = lax.all_to_all(payload.reshape(4, 8, *size), "x", 0, 0, tiled=True)
    parts = pl.pallas_call(
        partial_kernel,
        out_shape=shape(8, *size, dtype=BF16),
        in_specs=[VMEM],
        out_specs=VMEM,
        compiler_params=LIMIT,
        name="partial",
    )(parts)
    spread = pl.pallas_call(
        sum_kernel,
        out_shape=shape(8, *size, dtype=BF16),
        in_specs=[VMEM],
        out_specs=VMEM,
        compiler_params=LIMIT,
        name="total",
    )(lax.all_to_all(parts, "z", 0, 0, tiled=True))
    line = lax.all_to_all(spread, "z", 0, 0, tiled=True)
    whole = lax.all_to_all(jnp.broadcast_to(line[None], (4, 8, *size)), "x", 0, 0, tiled=True)
    return pl.pallas_call(
        final_kernel,
        out_shape=(shape(2 * HALF, K, dtype=BF16), shape(K, K), shape(CB * TILE, K)),
        in_specs=[SMEM] + [VMEM] * 3,
        out_specs=(VMEM, VMEM, VMEM),
        scratch_shapes=[pltpu.VMEM((K, 2 * K), F32)],
        compiler_params=LIMIT,
        name="finish",
    )(where, whole.reshape(PARTS, *size), mine, other)


def solution(mesh):
    grid = Mesh(mesh.devices.reshape(8, 4, 4, 2), ("z", "x", "y", "c"))
    row, col = ("z", "x"), ("y", "c")
    placed = (
        P(row, col, None, None, None),
        P(row, col, None),
        P(row, col, None),
        P(row, col),
        P(col, None),
    )
    return jax.shard_map(
        on_device,
        mesh=grid,
        in_specs=placed,
        out_specs=(P(row, None), P(), P(col, None)),
        check_vma=False,
    )
```

```python
import jax
import jax.numpy as jnp
from jax import lax
from jax.experimental import pallas as pl
from jax.experimental.pallas import tpu as pltpu
from jax.sharding import Mesh, PartitionSpec as P

F32 = jnp.float32
BF16 = jnp.bfloat16
TILE = 128
K = 256
RB = 16
CB = 16
SLOTS = 64
HALF = RB * TILE // 2
NROW = 65536
PARTS = 32
ROWS = CB * TILE // PARTS
EXTRA = 16
GROUP = 4
NB = 64
LOAD = 8
LIVE = 3
AT = 4
COLS = AT + SLOTS
PIECE = HALF // 4
VMEM = pl.BlockSpec(memory_space=pltpu.VMEM)
SMEM = pl.BlockSpec(memory_space=pltpu.SMEM)
HBM = pl.BlockSpec(memory_space=pltpu.HBM)


def dot(a, b, ca, cb, precision=None):
    return lax.dot_general(
        a, b, (((ca,), (cb,)), ((), ())), precision=precision, preferred_element_type=F32
    )


def iota(shape, dim):
    return lax.broadcasted_iota(jnp.int32, shape, dim)


def sketch_kernel(meta_ref, tiles_hbm, omega_hbm, keep_ref, send_ref, acc, tiles_ref, omega_ref, omega_sem, tile_sem):
    test = pltpu.make_async_copy(omega_hbm, omega_ref, omega_sem)
    big = [
        pltpu.make_async_copy(
            tiles_hbm.at[0, 0, pl.ds(g * LOAD, LOAD)], tiles_ref.at[pl.ds(g * LOAD, LOAD)], tile_sem.at[g]
        )
        for g in range(SLOTS // LOAD)
    ]
    big[0].start()
    test.start()
    for copy in big[1:]:
        copy.start()
    acc[...] = jnp.zeros_like(acc)
    live = meta_ref[LIVE]
    core, chip = meta_ref[0], meta_ref[1]
    test.wait()
    for g, copy in enumerate(big):
        copy.wait()

        @pl.when(g * LOAD < live)
        def _():
            prods, places = [], []
            for t in range(g * LOAD, (g + 1) * LOAD):
                prod = dot(tiles_ref[t], omega_ref[meta_ref[COLS + t] & (CB - 1)], 1, 0)
                prods.append(jnp.where(t < live, prod, 0.0))
                block = meta_ref[AT + t] & (RB - 1)
                half = (block // 8 + core) & 1
                places.append(half * 8 + ((block - 2 * chip) & 7))
            for prod, place in zip(prods, places):
                acc[place] += prod

    keep_ref[...] = acc[: RB // 2].reshape(HALF, K)
    send_ref[...] = acc[RB // 2 :].reshape(HALF, K)


def place_matrix(rows, cols, shift, dtype=BF16):
    e = iota((rows, cols), 0)
    p = iota((rows, cols), 1)
    return jnp.where((p // 6) * EXTRA + p % 6 + shift == e, 1.0, 0.0).astype(dtype)


def flip_kernel(meta_ref, tiles_ref, out_ref):
    live = meta_ref[LIVE]

    @pl.loop(0, SLOTS // GROUP)
    def _(g):
        for i in range(GROUP):
            t = g * GROUP + i
            tile = tiles_ref[t].T
            out_ref[t] = jnp.where(t < live, tile, jnp.zeros_like(tile))


def back_kernel(meta_ref, tiles_ref, mine_ref, other_ref, out_ref, s_ref, acc):
    core, chip = meta_ref[0], meta_ref[1]
    for k in range(4):
        at = ((chip - k) & 3) * 2
        part = pl.ds(k * PIECE, PIECE)
        s_ref[pl.ds(core * 8 + at, 2)] = mine_ref[part, :].reshape(2, TILE, K)
        s_ref[pl.ds((1 - core) * 8 + at, 2)] = other_ref[part, :].reshape(2, TILE, K)
    acc[...] = jnp.zeros_like(acc)

    @pl.loop(0, (meta_ref[LIVE] + LOAD - 1) // LOAD)
    def _(g):
        prods, places = [], []
        for i in range(LOAD):
            t = g * LOAD + i
            prods.append(dot(tiles_ref[t], s_ref[meta_ref[AT + t] & (RB - 1)], 1, 0))
            places.append(meta_ref[COLS + t] & (CB - 1))
        for prod, place in zip(prods, places):
            acc[place] += prod

    gram = dot(mine_ref[...], mine_ref[...], 0, 0) + dot(other_ref[...], other_ref[...], 0, 0)
    gram = gram * (1.0 / NROW)
    low = gram[K // 2 :, K // 2 :]
    low = jnp.concatenate([low[: K // 4], low[K // 4 :]], axis=1)
    packed = jnp.concatenate([gram[: K // 2], low], axis=0)
    high = packed.astype(BF16)
    rest = (packed - high.astype(F32)).astype(BF16)
    extra = dot(place_matrix(PARTS * EXTRA, 192, 0), high, 1, 0) + dot(
        place_matrix(PARTS * EXTRA, 192, 6), rest, 1, 0
    )
    out_ref[:, :ROWS, :] = acc[...].reshape(PARTS, ROWS, K).astype(BF16)
    out_ref[:, ROWS:, :] = extra.reshape(PARTS, EXTRA, K).astype(BF16)


def resplit(extra):
    row = iota(extra.shape, 0) % EXTRA
    gram = extra + pltpu.roll(extra, extra.shape[0] - 6, 0)
    high = gram.astype(BF16).astype(F32)
    low = pltpu.roll(gram - high, 6, 0)
    return jnp.where(row < 6, high, jnp.where(row < 12, low, 0.0))


def partial_kernel(in_ref, out_ref):
    total = in_ref[0].astype(F32)
    for i in range(1, 4):
        total = total + in_ref[i].astype(F32)
    out_ref[:, :ROWS, :] = total[:, :ROWS, :].astype(BF16)
    extra = resplit(total[:, ROWS:, :].reshape(8 * EXTRA, K))
    out_ref[:, ROWS:, :] = extra.reshape(8, EXTRA, K).astype(BF16)


def sum_kernel(in_ref, out_ref):
    total = in_ref[0].astype(F32)
    for i in range(1, 8):
        total = total + in_ref[i].astype(F32)
    w = total[:ROWS]
    mean = jnp.sum(w, axis=0, keepdims=True) * (1.0 / ROWS)
    top = jnp.max(jnp.abs(mean), axis=1, keepdims=True)
    lead = (mean / jnp.maximum(top, 1e-30)).astype(BF16)
    leadf = lead.astype(F32)
    norm = jnp.maximum(jnp.sum(leadf * leadf, axis=1, keepdims=True), 0.5)
    coef = (dot(lead, w.astype(BF16), 1, 1) / norm).astype(BF16)
    rest = w - dot(coef, lead, 0, 0)
    row = iota((EXTRA, K), 0)
    wide = jnp.concatenate([coef.astype(F32), jnp.zeros((1, K - ROWS), F32)], axis=1)
    tail = jnp.where(row == 12, leadf, jnp.where(row == 13, wide, resplit(total[ROWS:])))
    body = rest.astype(BF16)
    tail = tail.astype(BF16)
    for i in range(8):
        out_ref[i, :ROWS, :] = body
        out_ref[i, ROWS:, :] = tail


def eliminate(x):
    groups = NB // 8
    xs = [x[8 * g : 8 * g + 8] for g in range(groups)]
    sub = iota((8, 128), 0)

    def wide(a):
        return jnp.broadcast_to(a, (8, 128))

    for t in range(groups):
        at = 8 * t
        head = xs[t]
        cols = [wide(head[:, at + m : at + m + 1]) for m in range(8)]
        s = [[wide(cols[m][i : i + 1, :]) if m >= i else None for m in range(8)] for i in range(8)]
        rows = [wide(head[i : i + 1, :]) for i in range(8)]
        ratio = [[None] * 8 for _ in range(8)]
        scaled = []
        for j in range(8):
            inv = pltpu.reciprocal(s[j][j], approx=True)
            inv = inv * (2.0 - s[j][j] * inv)
            for m in range(j + 1, 8):
                ratio[j][m] = s[j][m] * inv
            for i in range(j + 1, 8):
                for m in range(i, 8):
                    s[i][m] = s[i][m] - ratio[j][i] * s[j][m]
                rows[i] = rows[i] - ratio[j][i] * rows[j]
            scaled.append(rows[j] * inv)
        for g in range(t + 1, groups):
            left, x = [], xs[g]
            for j in range(8):
                e = wide(xs[g][:, at + j : at + j + 1])
                for m in range(j):
                    e = e - ratio[m][j] * left[m]
                left.append(e)
                x = x - e * scaled[j]
            xs[g] = x
        out = rows[0] * lax.rsqrt(s[0][0])
        for j in range(1, 8):
            out = jnp.where(sub == j, rows[j] * lax.rsqrt(s[j][j]), out)
        xs[t] = out
    return jnp.concatenate(xs, axis=0)


def factor(work):
    lane = iota((NB, 128), 1)
    row = iota((NB, 128), 0)
    for b in range(K // NB):
        at = b * NB
        base = at // 128 * 128
        x = work[at : at + NB, base : base + 128]
        if at > base:
            x = pltpu.roll(x, 128 - (at - base), 1)
        x = eliminate(jnp.where(lane < NB, x, jnp.where(lane - NB == row, 1.0, 0.0)))
        inv = pltpu.roll(x, 128 - NB, 1)[:, :NB]
        u = dot(inv, work[at : at + NB, :], 1, 0, lax.Precision.HIGHEST)
        work[at : at + NB, :] = u
        if at + NB < K:
            ut = u[:, :K].T
            work[at + NB :, :] -= dot(ut[at + NB :], u, 1, 0, lax.Precision.HIGHEST)


def factor_kernel(meta_ref, e0_ref, e1_ref, e2_ref, e3_ref, mine_ref, other_ref,
                  q_ref, r_ref, inv_ref, lead_ref, coef_ref, work):
    extra = jnp.concatenate([e[...].reshape(8 * EXTRA, K) for e in (e0_ref, e1_ref, e2_ref, e3_ref)], axis=0)
    p = iota((192, PARTS * EXTRA), 0)
    e = iota((192, PARTS * EXTRA), 1)
    slot = p // 6
    first = (((meta_ref[2] - slot // 8) & 3) * 8 + slot % 8) * EXTRA + p % 6
    pick = jnp.where((e == first) | (e == first + 6), 1.0, 0.0).astype(BF16)
    packed = dot(pick, extra, 1, 0)
    work[: K // 2, :K] = packed[: K // 2]
    work[K // 2 :, : K // 2] = packed[: K // 2, K // 2 :].T
    work[K // 2 : 3 * K // 4, K // 2 : K] = packed[K // 2 :, : K // 2]
    work[3 * K // 4 :, K // 2 : K] = packed[K // 2 :, K // 2 :]
    work[:, K:] = jnp.where(iota((K, K), 0) == iota((K, K), 1), 1.0, 0.0)
    factor(work)
    r_ref[...] = jnp.where(iota((K, K), 0) <= iota((K, K), 1), work[:, :K], 0.0)
    inv = work[:, K:]
    high = inv.astype(BF16)
    low = (inv - high.astype(F32)).astype(BF16)
    inv_ref[:K, :] = high
    inv_ref[K:, :] = low
    i = iota((2 * PARTS, PARTS * EXTRA), 0)
    e = iota((2 * PARTS, PARTS * EXTRA), 1)
    want = jnp.where(i < PARTS, i * EXTRA + 12, (i - PARTS) * EXTRA + 13)
    leads = dot(jnp.where(e == want, 1.0, 0.0).astype(BF16), extra, 1, 0)
    lead = leads[:PARTS].astype(BF16)
    lead_ref[...] = dot(lead, high, 1, 1) + dot(lead, low, 1, 1)
    coef_ref[...] = leads[PARTS:, :TILE].T
    core, chip = meta_ref[0], meta_ref[1]
    for half, ref in ((core, mine_ref), (1 - core, other_ref)):
        for k in range(4):
            a = ref[k * PIECE : (k + 1) * PIECE, :]
            at = pl.multiple_of(half * HALF + ((chip - k) & 3) * PIECE, PIECE)
            q_ref[pl.ds(at, PIECE), :] = (dot(a, high, 1, 1) + dot(a, low, 1, 1)).astype(BF16)


def back_solve_kernel(meta_ref, b0_ref, b1_ref, b2_ref, b3_ref, inv_ref, lead_ref, coef_ref, z_hbm, z_ref, sem):
    copies = []
    for k, ref in enumerate((b0_ref, b1_ref, b2_ref, b3_ref)):
        a = ref[...].reshape(8 * ROWS, K)
        z = dot(a, inv_ref[:K, :], 1, 1) + dot(a, inv_ref[K:, :], 1, 1)
        for i in range(8):
            s = 8 * k + i
            term = coef_ref[:ROWS, s : s + 1] * lead_ref[s : s + 1, :]
            z_ref[k, i * ROWS : (i + 1) * ROWS, :] = z[i * ROWS : (i + 1) * ROWS] + term
        at = pl.multiple_of(((meta_ref[2] - k) & 3) * 8 * ROWS, 8 * ROWS)
        copy = pltpu.make_async_copy(z_ref.at[k], z_hbm.at[pl.ds(at, 8 * ROWS), :], sem.at[k])
        copy.start()
        copies.append(copy)
    for copy in copies:
        copy.wait()


def shape(*dims, dtype=F32):
    return jax.ShapeDtypeStruct(dims, dtype)


LIMIT = pltpu.CompilerParams(vmem_limit_bytes=40 * 1024 * 1024)


def on_device(tiles, block_rows, block_cols, tile_counts, omega):
    places = [lax.axis_index(axis).astype(jnp.int32).reshape(1) for axis in ("c", "y", "x")]
    meta = jnp.concatenate(places + [tile_counts[0], block_rows[0, 0], block_cols[0, 0]])
    swap = [(0, 1), (1, 0)]
    keep, send = pl.pallas_call(
        sketch_kernel,
        out_shape=(shape(HALF, K), shape(HALF, K)),
        in_specs=[SMEM] + [HBM] * 2,
        out_specs=(VMEM, VMEM),
        scratch_shapes=[
            pltpu.VMEM((RB, TILE, K), F32),
            pltpu.VMEM((SLOTS, TILE, TILE), BF16),
            pltpu.VMEM((CB, TILE, K), BF16),
            pltpu.SemaphoreType.DMA,
            pltpu.SemaphoreType.DMA((SLOTS // LOAD,)),
        ],
        compiler_params=pltpu.CompilerParams(vmem_limit_bytes=51 * 1024 * 1024),
        name="sketch",
    )(meta, tiles, omega.reshape(CB, TILE, K))

    def turn(a, k, axis="y"):
        return lax.ppermute(a, axis, [(i, (i + k) % 4) for i in range(4)])

    half = keep + lax.ppermute(send, "c", swap)
    quarters = half.reshape(4, PIECE, K)
    sent = [quarters[k].astype(BF16) for k in range(4)]
    sent[2], later = lax.optimization_barrier((sent[2], meta))
    flipped = pl.pallas_call(
        flip_kernel,
        out_shape=shape(SLOTS, TILE, TILE, dtype=BF16),
        in_specs=[SMEM, VMEM],
        out_specs=VMEM,
        compiler_params=LIMIT,
        cost_estimate=pl.CostEstimate(flops=4 * 10**9, bytes_accessed=4 * 2**20, transcendentals=0),
        name="flip",
    )(later, tiles[0, 0])
    shard = quarters[0]
    for k in (2, 1, 3):
        shard = shard + turn(sent[k], k).astype(F32)
    shard, flipped = lax.optimization_barrier((shard.astype(BF16), flipped))
    mine = jnp.concatenate([shard] + [turn(shard, k) for k in (1, 2, 3)], axis=0)
    other = lax.ppermute(mine, "c", swap)
    payload = pl.pallas_call(
        back_kernel,
        out_shape=shape(PARTS, ROWS + EXTRA, K, dtype=BF16),
        in_specs=[SMEM] + [VMEM] * 3,
        out_specs=VMEM,
        scratch_shapes=[pltpu.VMEM((RB, TILE, K), BF16), pltpu.VMEM((CB, TILE, K), F32)],
        compiler_params=LIMIT,
        name="back",
    )(meta, flipped, mine, other)
    size = (ROWS + EXTRA, K)
    parts = lax.all_to_all(payload.reshape(4, 8, *size), "x", 0, 0, tiled=True)
    parts = pl.pallas_call(
        partial_kernel,
        out_shape=shape(8, *size, dtype=BF16),
        in_specs=[VMEM],
        out_specs=VMEM,
        compiler_params=LIMIT,
        name="partial",
    )(parts)
    spread = pl.pallas_call(
        sum_kernel,
        out_shape=shape(8, *size, dtype=BF16),
        in_specs=[VMEM],
        out_specs=VMEM,
        compiler_params=LIMIT,
        name="total",
    )(lax.all_to_all(parts, "z", 0, 0, tiled=True))
    line = lax.all_to_all(spread, "z", 0, 0, tiled=True)
    body, extra = line[:, :ROWS, :], line[:, ROWS:, :]
    extras = [extra] + [turn(extra, k, "x") for k in (2, 1, 3)]
    bodies = [body] + [turn(body, k, "x") for k in (2, 1, 3)]
    extras = [extras[0], extras[2], extras[1], extras[3]]
    bodies = [bodies[0], bodies[2], bodies[1], bodies[3]]
    q, r, inv, lead, coef = pl.pallas_call(
        factor_kernel,
        out_shape=(
            shape(2 * HALF, K, dtype=BF16),
            shape(K, K),
            shape(2 * K, K, dtype=BF16),
            shape(PARTS, K),
            shape(TILE, PARTS),
        ),
        in_specs=[SMEM] + [VMEM] * 6,
        out_specs=(VMEM,) * 5,
        scratch_shapes=[pltpu.VMEM((K, 2 * K), F32)],
        compiler_params=LIMIT,
        cost_estimate=pl.CostEstimate(flops=12 * 10**9, bytes_accessed=4 * 2**20, transcendentals=0),
        name="factor",
    )(meta, *extras, mine, other)
    z = pl.pallas_call(
        back_solve_kernel,
        out_shape=shape(CB * TILE, K),
        in_specs=[SMEM] + [VMEM] * 7,
        out_specs=HBM,
        scratch_shapes=[pltpu.VMEM((4, 8 * ROWS, K), F32), pltpu.SemaphoreType.DMA((4,))],
        compiler_params=LIMIT,
        name="z",
    )(meta, *bodies, inv, lead, coef)
    return q, r, z


def solution(mesh):
    grid = Mesh(mesh.devices.reshape(8, 4, 4, 2), ("z", "x", "y", "c"))
    row, col = ("z", "x"), ("y", "c")
    placed = (
        P(row, col, None, None, None),
        P(row, col, None),
        P(row, col, None),
        P(row, col),
        P(col, None),
    )
    return jax.shard_map(
        on_device,
        mesh=grid,
        in_specs=placed,
        out_specs=(P(row, None), P(), P(col, None)),
        check_vma=False,
    )
```

```python
import functools

import jax
import jax.numpy as jnp
from jax import lax
from jax.experimental import pallas as pl
from jax.experimental.pallas import tpu as pltpu
from jax.sharding import Mesh, PartitionSpec as P

F32 = jnp.float32
BF16 = jnp.bfloat16
TILE = 128
K = 256
RB = 16
CB = 16
SLOTS = 64
HALF = RB * TILE // 2
NROW = 65536
PARTS = 32
ROWS = CB * TILE // PARTS
EXTRA = 16
GROUP = 4
NB = 64
LOAD = 8
LIVE = 3
AT = 4
COLS = AT + SLOTS
START = COLS + SLOTS
PIECE = HALF // 4
VMEM = pl.BlockSpec(memory_space=pltpu.VMEM)
SMEM = pl.BlockSpec(memory_space=pltpu.SMEM)
HBM = pl.BlockSpec(memory_space=pltpu.HBM)


def dot(a, b, ca, cb, precision=None):
    return lax.dot_general(
        a, b, (((ca,), (cb,)), ((), ())), precision=precision, preferred_element_type=F32
    )


def iota(shape, dim):
    return lax.broadcasted_iota(jnp.int32, shape, dim)


def sketch_kernel(meta_ref, tiles_hbm, omega_hbm, keep_ref, send_ref, acc, tiles_ref, omega_ref, omega_sem, tile_sem):
    test = pltpu.make_async_copy(omega_hbm, omega_ref, omega_sem)
    big = [
        pltpu.make_async_copy(
            tiles_hbm.at[0, 0, pl.ds(g * LOAD, LOAD)], tiles_ref.at[pl.ds(g * LOAD, LOAD)], tile_sem.at[g]
        )
        for g in range(SLOTS // LOAD)
    ]
    big[0].start()
    test.start()
    for copy in big[1:]:
        copy.start()
    acc[...] = jnp.zeros_like(acc)
    live = meta_ref[LIVE]
    core, chip = meta_ref[0], meta_ref[1]
    test.wait()
    for g, copy in enumerate(big):
        copy.wait()

        @pl.when(g * LOAD < live)
        def _():
            prods, places = [], []
            for t in range(g * LOAD, (g + 1) * LOAD):
                prod = dot(tiles_ref[t], omega_ref[meta_ref[COLS + t] & (CB - 1)], 1, 0)
                prods.append(jnp.where(t < live, prod, 0.0))
                block = meta_ref[AT + t] & (RB - 1)
                half = (block // 8 + core) & 1
                places.append(half * 8 + ((block - 2 * chip) & 7))
            for prod, place in zip(prods, places):
                acc[place] += prod

    keep_ref[...] = acc[: RB // 2].reshape(HALF, K)
    send_ref[...] = acc[RB // 2 :].reshape(HALF, K)


def flip_kernel(meta_ref, tiles_ref, out_ref, sorted_ref, count, source):
    live = meta_ref[LIVE]
    for i in range(8):
        count[i] = 0
    for i in range(3):
        sorted_ref[i] = meta_ref[i]

    def turned(t):
        return (meta_ref[COLS + t] - 4 * meta_ref[2]) & (CB - 1)

    def chunk(t):
        return jnp.where(t < live, turned(t) // 4, 4)

    @pl.loop(0, SLOTS)
    def _(t):
        c = chunk(t)
        count[c] = count[c] + 1

    begin = jnp.int32(0)
    for i in range(5):
        here = count[i]
        sorted_ref[START + i] = begin
        count[i] = begin
        begin = begin + here

    @pl.loop(0, SLOTS)
    def _(t):
        c = chunk(t)
        at = count[c]
        count[c] = at + 1
        source[at] = t
        sorted_ref[AT + at] = meta_ref[AT + t] & (RB - 1)
        sorted_ref[COLS + at] = turned(t)

    @pl.loop(0, SLOTS // GROUP)
    def _(g):
        for i in range(GROUP):
            t = g * GROUP + i
            tile = tiles_ref[source[t]].T
            out_ref[t] = jnp.where(t < live, tile, jnp.zeros_like(tile))


def gram_kernel(mine_ref, out_ref):
    out_ref[...] = dot(mine_ref[...], mine_ref[...], 0, 0)


def slab_kernel(meta_ref, mine_ref, other_ref, gram_ref, s_ref, g0_ref, g1_ref, g2_ref, g3_ref):
    core, chip, x = meta_ref[0], meta_ref[1], meta_ref[2]
    for k in range(4):
        at = ((chip - k) & 3) * 2
        part = pl.ds(k * PIECE, PIECE)
        s_ref[pl.ds(core * 8 + at, 2)] = mine_ref[part, :].reshape(2, TILE, K)
        s_ref[pl.ds((1 - core) * 8 + at, 2)] = other_ref[part, :].reshape(2, TILE, K)
    gram = (gram_ref[...] + dot(other_ref[...], other_ref[...], 0, 0)) * (1.0 / NROW)
    low = gram[K // 2 :, K // 2 :]
    low = jnp.concatenate([low[: K // 4], low[K // 4 :]], axis=1)
    packed = jnp.concatenate([gram[: K // 2], low], axis=0)
    high = packed.astype(BF16)
    rest = (packed - high.astype(F32)).astype(BF16)
    e = iota((PARTS * EXTRA, 192), 0)
    p = iota((PARTS * EXTRA, 192), 1)
    slot = p // 6
    first = (((slot // 8 - x) & 3) * 8 + slot % 8) * EXTRA + p % 6
    extra = dot(jnp.where(e == first, 1.0, 0.0).astype(BF16), high, 1, 0) + dot(
        jnp.where(e == first + 6, 1.0, 0.0).astype(BF16), rest, 1, 0
    )
    for k, ref in enumerate((g0_ref, g1_ref, g2_ref, g3_ref)):
        ref[...] = extra[k * 8 * EXTRA : (k + 1) * 8 * EXTRA].reshape(8, EXTRA, K).astype(BF16)


def back_kernel(first, last, meta_ref, tiles_ref, s_ref, *refs):
    *out_refs, acc = refs
    begin, end = meta_ref[START + first], meta_ref[START + last + 1]
    acc[...] = jnp.zeros_like(acc)

    @pl.loop(0, (end - begin + LOAD - 1) // LOAD)
    def _(g):
        prods, places = [], []
        for i in range(LOAD):
            t = begin + g * LOAD + i
            safe = jnp.minimum(t, SLOTS - 1)
            prod = dot(tiles_ref[safe], s_ref[meta_ref[AT + safe]], 1, 0)
            prods.append(jnp.where(t < end, prod, 0.0))
            places.append(jnp.where(t < end, meta_ref[COLS + safe] - 4 * first, 0))
        for prod, place in zip(prods, places):
            acc[place] += prod

    for k, ref in enumerate(out_refs):
        ref[...] = acc[4 * k : 4 * k + 4].reshape(8, ROWS, K).astype(BF16)


def resplit(extra):
    row = iota(extra.shape, 0) % EXTRA
    gram = extra + pltpu.roll(extra, extra.shape[0] - 6, 0)
    high = gram.astype(BF16).astype(F32)
    low = pltpu.roll(gram - high, 6, 0)
    return jnp.where(row < 6, high, jnp.where(row < 12, low, 0.0))


def gram_sum_kernel(a_ref, b_ref, c_ref, d_ref, out_ref):
    total = jnp.zeros((8 * EXTRA, K), F32)
    for ref in (a_ref, b_ref, c_ref, d_ref):
        total = total + ref[...].reshape(8 * EXTRA, K).astype(F32)
    out_ref[...] = resplit(total).reshape(8, EXTRA, K).astype(BF16)


def partial_kernel(a_ref, b_ref, c_ref, d_ref, gram_ref, out_ref):
    total = a_ref[...].astype(F32)
    for ref in (b_ref, c_ref, d_ref):
        total = total + ref[...].astype(F32)
    out_ref[:, :ROWS, :] = total.astype(BF16)
    gram = gram_ref[0].astype(F32)
    for i in range(1, 8):
        gram = gram + gram_ref[i].astype(F32)
    gram = resplit(gram).astype(BF16)
    for i in range(8):
        out_ref[i, ROWS:, :] = gram


def sum_kernel(in_ref, out_ref, gram_ref):
    w = in_ref[0, :ROWS, :].astype(F32)
    for i in range(1, 8):
        w = w + in_ref[i, :ROWS, :].astype(F32)
    gram_ref[...] = in_ref[:, ROWS:, :]
    mean = jnp.sum(w, axis=0, keepdims=True) * (1.0 / ROWS)
    top = jnp.max(jnp.abs(mean), axis=1, keepdims=True)
    lead = (mean / jnp.maximum(top, 1e-30)).astype(BF16)
    leadf = lead.astype(F32)
    norm = jnp.maximum(jnp.sum(leadf * leadf, axis=1, keepdims=True), 0.5)
    coef = (dot(lead, w.astype(BF16), 1, 1) / norm).astype(BF16)
    rest = w - dot(coef, lead, 0, 0)
    row = iota((EXTRA, K), 0)
    wide = jnp.concatenate([coef.astype(F32), jnp.zeros((1, K - ROWS), F32)], axis=1)
    tail = jnp.where(row == 0, leadf, jnp.where(row == 1, wide, 0.0)).astype(BF16)
    body = rest.astype(BF16)
    for i in range(8):
        out_ref[i, :ROWS, :] = body
        out_ref[i, ROWS:, :] = tail


def eliminate(x):
    groups = NB // 8
    xs = [x[8 * g : 8 * g + 8] for g in range(groups)]
    sub = iota((8, 128), 0)

    def wide(a):
        return jnp.broadcast_to(a, (8, 128))

    for t in range(groups):
        at = 8 * t
        head = xs[t]
        cols = [wide(head[:, at + m : at + m + 1]) for m in range(8)]
        s = [[wide(cols[m][i : i + 1, :]) if m >= i else None for m in range(8)] for i in range(8)]
        rows = [wide(head[i : i + 1, :]) for i in range(8)]
        ratio = [[None] * 8 for _ in range(8)]
        scaled = []
        for j in range(8):
            inv = pltpu.reciprocal(s[j][j], approx=True)
            inv = inv * (2.0 - s[j][j] * inv)
            for m in range(j + 1, 8):
                ratio[j][m] = s[j][m] * inv
            for i in range(j + 1, 8):
                for m in range(i, 8):
                    s[i][m] = s[i][m] - ratio[j][i] * s[j][m]
                rows[i] = rows[i] - ratio[j][i] * rows[j]
            scaled.append(rows[j] * inv)
        for g in range(t + 1, groups):
            left, x = [], xs[g]
            for j in range(8):
                e = wide(xs[g][:, at + j : at + j + 1])
                for m in range(j):
                    e = e - ratio[m][j] * left[m]
                left.append(e)
                x = x - e * scaled[j]
            xs[g] = x
        out = rows[0] * lax.rsqrt(s[0][0])
        for j in range(1, 8):
            out = jnp.where(sub == j, rows[j] * lax.rsqrt(s[j][j]), out)
        xs[t] = out
    return jnp.concatenate(xs, axis=0)


def factor(work):
    lane = iota((NB, 128), 1)
    row = iota((NB, 128), 0)
    for b in range(K // NB):
        at = b * NB
        base = at // 128 * 128
        x = work[at : at + NB, base : base + 128]
        if at > base:
            x = pltpu.roll(x, 128 - (at - base), 1)
        x = eliminate(jnp.where(lane < NB, x, jnp.where(lane - NB == row, 1.0, 0.0)))
        inv = pltpu.roll(x, 128 - NB, 1)[:, :NB]
        u = dot(inv, work[at : at + NB, :], 1, 0, lax.Precision.HIGHEST)
        work[at : at + NB, :] = u
        if at + NB < K:
            ut = u[:, :K].T
            work[at + NB :, :] -= dot(ut[at + NB :], u, 1, 0, lax.Precision.HIGHEST)


def factor_kernel(meta_ref, e0_ref, e1_ref, e2_ref, e3_ref, s_ref, q_ref, r_ref, inv_ref, work):
    extra = jnp.concatenate([e[...].reshape(8 * EXTRA, K) for e in (e0_ref, e1_ref, e2_ref, e3_ref)], axis=0)
    p = iota((192, PARTS * EXTRA), 0)
    e = iota((192, PARTS * EXTRA), 1)
    slot = p // 6
    first = (((meta_ref[2] - slot // 8) & 3) * 8 + slot % 8) * EXTRA + p % 6
    pick = jnp.where((e == first) | (e == first + 6), 1.0, 0.0).astype(BF16)
    packed = dot(pick, extra, 1, 0)
    work[: K // 2, :K] = packed[: K // 2]
    work[K // 2 :, : K // 2] = packed[: K // 2, K // 2 :].T
    work[K // 2 : 3 * K // 4, K // 2 : K] = packed[K // 2 :, : K // 2]
    work[3 * K // 4 :, K // 2 : K] = packed[K // 2 :, K // 2 :]
    work[:, K:] = jnp.where(iota((K, K), 0) == iota((K, K), 1), 1.0, 0.0)
    factor(work)
    r_ref[...] = jnp.where(iota((K, K), 0) <= iota((K, K), 1), work[:, :K], 0.0)
    inv = work[:, K:]
    high = inv.astype(BF16)
    low = (inv - high.astype(F32)).astype(BF16)
    inv_ref[:K, :] = high
    inv_ref[K:, :] = low
    for k in range(4):
        a = s_ref[4 * k : 4 * k + 4].reshape(4 * TILE, K)
        q_ref[k * 4 * TILE : (k + 1) * 4 * TILE, :] = (dot(a, high, 1, 1) + dot(a, low, 1, 1)).astype(BF16)


def back_solve_kernel(meta_ref, b0_ref, b1_ref, b2_ref, b3_ref, inv_ref, z_hbm, z_ref, sem):
    i = iota((EXTRA, 8 * EXTRA), 0)
    e = iota((EXTRA, 8 * EXTRA), 1)
    pick = jnp.where(e == (i % 8) * EXTRA + i // 8, 1.0, 0.0).astype(BF16)
    copies = []
    for k, ref in enumerate((b0_ref, b1_ref, b2_ref, b3_ref)):
        leads = dot(pick, ref[:, ROWS:, :].reshape(8 * EXTRA, K), 1, 0)
        lead = leads[:8].astype(BF16)
        lead = dot(lead, inv_ref[:K, :], 1, 1) + dot(lead, inv_ref[K:, :], 1, 1)
        coef = leads[8:, :TILE].T
        a = ref[:, :ROWS, :].reshape(8 * ROWS, K)
        z = dot(a, inv_ref[:K, :], 1, 1) + dot(a, inv_ref[K:, :], 1, 1)
        for s in range(8):
            z_ref[k, s * ROWS : (s + 1) * ROWS, :] = (
                z[s * ROWS : (s + 1) * ROWS] + coef[:ROWS, s : s + 1] * lead[s : s + 1, :]
            )
        at = pl.multiple_of(((meta_ref[2] - k) & 3) * 8 * ROWS, 8 * ROWS)
        copy = pltpu.make_async_copy(z_ref.at[k], z_hbm.at[pl.ds(at, 8 * ROWS), :], sem.at[k])
        copy.start()
        copies.append(copy)
    for copy in copies:
        copy.wait()


def shape(*dims, dtype=F32):
    return jax.ShapeDtypeStruct(dims, dtype)


def cost(us):
    return pl.CostEstimate(flops=us * 10**9, bytes_accessed=2**20, transcendentals=0)


LIMIT = pltpu.CompilerParams(vmem_limit_bytes=40 * 1024 * 1024)


def on_device(tiles, block_rows, block_cols, tile_counts, omega):
    places = [lax.axis_index(axis).astype(jnp.int32).reshape(1) for axis in ("c", "y", "x")]
    meta = jnp.concatenate(places + [tile_counts[0], block_rows[0, 0], block_cols[0, 0]])
    swap = [(0, 1), (1, 0)]
    keep, send = pl.pallas_call(
        sketch_kernel,
        out_shape=(shape(HALF, K), shape(HALF, K)),
        in_specs=[SMEM] + [HBM] * 2,
        out_specs=(VMEM, VMEM),
        scratch_shapes=[
            pltpu.VMEM((RB, TILE, K), F32),
            pltpu.VMEM((SLOTS, TILE, TILE), BF16),
            pltpu.VMEM((CB, TILE, K), BF16),
            pltpu.SemaphoreType.DMA,
            pltpu.SemaphoreType.DMA((SLOTS // LOAD,)),
        ],
        compiler_params=pltpu.CompilerParams(vmem_limit_bytes=51 * 1024 * 1024),
        name="sketch",
    )(meta, tiles, omega.reshape(CB, TILE, K))

    def turn(a, k, axis="y"):
        return lax.ppermute(a, axis, [(i, (i + k) % 4) for i in range(4)])

    half = keep + lax.ppermute(send, "c", swap)
    quarters = half.reshape(4, PIECE, K)
    sent = [quarters[k].astype(BF16) for k in range(4)]
    sent[2], later = lax.optimization_barrier((sent[2], meta))
    flipped, order = pl.pallas_call(
        flip_kernel,
        out_shape=(shape(SLOTS, TILE, TILE, dtype=BF16), shape(START + 8, dtype=jnp.int32)),
        in_specs=[SMEM, VMEM],
        out_specs=(VMEM, SMEM),
        scratch_shapes=[pltpu.SMEM((8,), jnp.int32), pltpu.SMEM((SLOTS,), jnp.int32)],
        compiler_params=LIMIT,
        cost_estimate=cost(4),
        name="flip",
    )(later, tiles[0, 0])
    shard = quarters[0]
    for k in (2, 1, 3):
        shard = shard + turn(sent[k], k).astype(F32)
    shard, flipped = lax.optimization_barrier((shard.astype(BF16), flipped))
    mine = jnp.concatenate([shard] + [turn(shard, k) for k in (1, 2, 3)], axis=0)
    other = lax.ppermute(mine, "c", swap)
    half_gram = pl.pallas_call(
        gram_kernel,
        out_shape=shape(K, K),
        in_specs=[VMEM],
        out_specs=VMEM,
        compiler_params=LIMIT,
        cost_estimate=cost(1),
        name="gram",
    )(mine)
    slab, *grams = pl.pallas_call(
        slab_kernel,
        out_shape=(shape(RB, TILE, K, dtype=BF16),) + (shape(8, EXTRA, K, dtype=BF16),) * 4,
        in_specs=[SMEM] + [VMEM] * 3,
        out_specs=(VMEM,) * 5,
        compiler_params=LIMIT,
        cost_estimate=cost(1),
        name="slab",
    )(meta, mine, other, half_gram)
    grams = [grams[0]] + [turn(grams[k], k, "x") for k in (1, 2, 3)]
    backs = []
    for first, last in ((1, 3), (0, 0)):
        count = last - first + 1
        backs += pl.pallas_call(
            functools.partial(back_kernel, first, last),
            out_shape=(shape(8, ROWS, K, dtype=BF16),) * count,
            in_specs=[SMEM] + [VMEM] * 2,
            out_specs=(VMEM,) * count,
            scratch_shapes=[pltpu.VMEM((4 * count, TILE, K), F32)],
            compiler_params=LIMIT,
            cost_estimate=cost(10 if first else 1),
            name=f"back{first}",
        )(order, flipped, slab)
    backs = [backs[3]] + [turn(backs[k - 1], k, "x") for k in (1, 2, 3)]
    grams = pl.pallas_call(
        gram_sum_kernel,
        out_shape=shape(8, EXTRA, K, dtype=BF16),
        in_specs=[VMEM] * 4,
        out_specs=VMEM,
        compiler_params=LIMIT,
        name="gram_sum",
    )(*grams)
    grams = lax.all_to_all(grams, "z", 0, 0, tiled=True)
    size = (ROWS + EXTRA, K)
    parts = pl.pallas_call(
        partial_kernel,
        out_shape=shape(8, *size, dtype=BF16),
        in_specs=[VMEM] * 5,
        out_specs=VMEM,
        compiler_params=LIMIT,
        name="partial",
    )(*backs, grams)
    spread, gram = pl.pallas_call(
        sum_kernel,
        out_shape=(shape(8, *size, dtype=BF16), shape(8, EXTRA, K, dtype=BF16)),
        in_specs=[VMEM],
        out_specs=(VMEM, VMEM),
        compiler_params=LIMIT,
        name="total",
    )(lax.all_to_all(parts, "z", 0, 0, tiled=True))
    extras = [gram] + [turn(gram, k, "x") for k in (1, 2, 3)]
    line = lax.all_to_all(spread, "z", 0, 0, tiled=True)
    bodies = [line] + [turn(line, k, "x") for k in (1, 2, 3)]
    q, r, inv = pl.pallas_call(
        factor_kernel,
        out_shape=(shape(2 * HALF, K, dtype=BF16), shape(K, K), shape(2 * K, K, dtype=BF16)),
        in_specs=[SMEM] + [VMEM] * 5,
        out_specs=(VMEM,) * 3,
        scratch_shapes=[pltpu.VMEM((K, 2 * K), F32)],
        compiler_params=LIMIT,
        cost_estimate=cost(13),
        name="factor",
    )(meta, *extras, slab)
    z = pl.pallas_call(
        back_solve_kernel,
        out_shape=shape(CB * TILE, K),
        in_specs=[SMEM] + [VMEM] * 5,
        out_specs=HBM,
        scratch_shapes=[pltpu.VMEM((4, 8 * ROWS, K), F32), pltpu.SemaphoreType.DMA((4,))],
        compiler_params=LIMIT,
        name="z",
    )(meta, *bodies, inv)
    return q, r, z


def solution(mesh):
    grid = Mesh(mesh.devices.reshape(8, 4, 4, 2), ("z", "x", "y", "c"))
    row, col = ("z", "x"), ("y", "c")
    placed = (
        P(row, col, None, None, None),
        P(row, col, None),
        P(row, col, None),
        P(row, col),
        P(col, None),
    )
    return jax.shard_map(
        on_device,
        mesh=grid,
        in_specs=placed,
        out_specs=(P(row, None), P(), P(col, None)),
        check_vma=False,
    )
```

```python
import functools

import jax
import jax.numpy as jnp
from jax import lax
from jax.experimental import pallas as pl
from jax.experimental.pallas import tpu as pltpu
from jax.sharding import Mesh, PartitionSpec as P

F32 = jnp.float32
BF16 = jnp.bfloat16
TILE = 128
K = 256
RB = 16
CB = 16
SLOTS = 64
HALF = RB * TILE // 2
NROW = 65536
PARTS = 32
ROWS = CB * TILE // PARTS
EXTRA = 16
TAIL = 8
GROUP = 4
NB = 64
FIRST = 1
LOAD = 8
LIVE = 3
AT = 4
COLS = AT + SLOTS
START = COLS + SLOTS
SOURCE = START + 8
PIECE = HALF // 4
VMEM = pl.BlockSpec(memory_space=pltpu.VMEM)
SMEM = pl.BlockSpec(memory_space=pltpu.SMEM)
HBM = pl.BlockSpec(memory_space=pltpu.HBM)


def dot(a, b, ca, cb, precision=None):
    return lax.dot_general(
        a, b, (((ca,), (cb,)), ((), ())), precision=precision, preferred_element_type=F32
    )


def iota(shape, dim):
    return lax.broadcasted_iota(jnp.int32, shape, dim)


def sketch_kernel(meta_ref, tiles_hbm, omega_hbm, keep_ref, send_ref, acc, tiles_ref, omega_ref, omega_sem, tile_sem):
    test = pltpu.make_async_copy(omega_hbm, omega_ref, omega_sem)
    big = [
        pltpu.make_async_copy(
            tiles_hbm.at[0, 0, pl.ds(g * LOAD, LOAD)], tiles_ref.at[pl.ds(g * LOAD, LOAD)], tile_sem.at[g]
        )
        for g in range(SLOTS // LOAD)
    ]
    big[0].start()
    test.start()
    for copy in big[1:]:
        copy.start()
    acc[...] = jnp.zeros_like(acc)
    live = meta_ref[LIVE]
    core, chip = meta_ref[0], meta_ref[1]
    test.wait()
    for g, copy in enumerate(big):
        copy.wait()

        @pl.when(g * LOAD < live)
        def _():
            prods, places = [], []
            for t in range(g * LOAD, (g + 1) * LOAD):
                prod = dot(tiles_ref[t], omega_ref[meta_ref[COLS + t] & (CB - 1)], 1, 0)
                prods.append(jnp.where(t < live, prod, 0.0))
                block = meta_ref[AT + t] & (RB - 1)
                half = (block // 8 + core) & 1
                places.append(half * 8 + ((block - 2 * chip) & 7))
            for prod, place in zip(prods, places):
                acc[place] += prod

    keep_ref[...] = acc[: RB // 2].reshape(HALF, K)
    send_ref[...] = acc[RB // 2 :].reshape(HALF, K).astype(BF16)


def order_kernel(meta_ref, sorted_ref, count):
    live = meta_ref[LIVE]
    for i in range(8):
        count[i] = 0
    for i in range(3):
        sorted_ref[i] = meta_ref[i]

    def turned(t):
        return (meta_ref[COLS + t] - 4 * meta_ref[2]) & (CB - 1)

    def chunk(t):
        return jnp.where(t < live, turned(t) // 4, 4)

    @pl.loop(0, SLOTS)
    def _(t):
        c = chunk(t)
        count[c] = count[c] + 1

    begin = jnp.int32(0)
    for i in range(5):
        here = count[i]
        sorted_ref[START + i] = begin
        count[i] = begin
        begin = begin + here

    @pl.loop(0, SLOTS)
    def _(t):
        c = chunk(t)
        at = count[c]
        count[c] = at + 1
        sorted_ref[SOURCE + at] = t
        sorted_ref[AT + at] = meta_ref[AT + t] & (RB - 1)
        sorted_ref[COLS + at] = turned(t)


def flip_kernel(meta_ref, tiles_ref, out_ref):
    @pl.loop(0, SLOTS // GROUP)
    def _(g):
        for i in range(GROUP):
            t = g * GROUP + i
            out_ref[t] = tiles_ref[meta_ref[SOURCE + t]].T


def gram_kernel(mine_ref, out_ref):
    out_ref[...] = dot(mine_ref[...], mine_ref[...], 0, 0)


def slab_kernel(meta_ref, mine_ref, other_ref, gram_ref, s_ref, g0_ref, g1_ref, g2_ref, g3_ref):
    core, chip, x = meta_ref[0], meta_ref[1], meta_ref[2]
    for k in range(4):
        at = ((chip - k) & 3) * 2
        part = pl.ds(k * PIECE, PIECE)
        s_ref[pl.ds(core * 8 + at, 2)] = mine_ref[part, :].reshape(2, TILE, K)
        s_ref[pl.ds((1 - core) * 8 + at, 2)] = other_ref[part, :].reshape(2, TILE, K)
    gram = (gram_ref[...] + dot(other_ref[...], other_ref[...], 0, 0)) * (1.0 / NROW)
    low = gram[K // 2 :, K // 2 :]
    low = jnp.concatenate([low[: K // 4], low[K // 4 :]], axis=1)
    packed = jnp.concatenate([gram[: K // 2], low], axis=0)
    high = packed.astype(BF16)
    rest = (packed - high.astype(F32)).astype(BF16)
    e = iota((PARTS * EXTRA, 192), 0)
    p = iota((PARTS * EXTRA, 192), 1)
    slot = p // 6
    first = (((slot // 8 - x) & 3) * 8 + slot % 8) * EXTRA + p % 6
    extra = dot(jnp.where(e == first, 1.0, 0.0).astype(BF16), high, 1, 0) + dot(
        jnp.where(e == first + 6, 1.0, 0.0).astype(BF16), rest, 1, 0
    )
    for k, ref in enumerate((g0_ref, g1_ref, g2_ref, g3_ref)):
        ref[...] = extra[k * 8 * EXTRA : (k + 1) * 8 * EXTRA].reshape(8, EXTRA, K).astype(BF16)


def back_kernel(first, last, meta_ref, tiles_ref, s_ref, *refs):
    *out_refs, acc = refs
    begin, end = meta_ref[START + first], meta_ref[START + last + 1]
    acc[...] = jnp.zeros_like(acc)

    @pl.loop(0, (end - begin + LOAD - 1) // LOAD)
    def _(g):
        prods, places = [], []
        for i in range(LOAD):
            t = begin + g * LOAD + i
            safe = jnp.minimum(t, SLOTS - 1)
            prod = dot(tiles_ref[safe], s_ref[meta_ref[AT + safe]], 1, 0)
            prods.append(jnp.where(t < end, prod, 0.0))
            places.append(jnp.where(t < end, meta_ref[COLS + safe] - 4 * first, 0))
        for prod, place in zip(prods, places):
            acc[place] += prod

    for k, ref in enumerate(out_refs):
        ref[...] = acc[4 * k : 4 * k + 4].reshape(8, ROWS, K).astype(BF16)


def resplit(extra):
    row = iota(extra.shape, 0) % EXTRA
    gram = extra + pltpu.roll(extra, extra.shape[0] - 6, 0)
    high = gram.astype(BF16).astype(F32)
    low = pltpu.roll(gram - high, 6, 0)
    return jnp.where(row < 6, high, jnp.where(row < 12, low, 0.0))


def gram_sum_kernel(a_ref, b_ref, c_ref, d_ref, out_ref):
    total = jnp.zeros((8 * EXTRA, K), F32)
    for ref in (a_ref, b_ref, c_ref, d_ref):
        total = total + ref[...].reshape(8 * EXTRA, K).astype(F32)
    out_ref[...] = resplit(total).reshape(8, EXTRA, K).astype(BF16)


def partial_kernel(a_ref, b_ref, c_ref, d_ref, gram_ref, out_ref):
    total = a_ref[...].astype(F32)
    for ref in (b_ref, c_ref, d_ref):
        total = total + ref[...].astype(F32)
    out_ref[:, :ROWS, :] = total.astype(BF16)
    gram = gram_ref[0].astype(F32)
    for i in range(1, 8):
        gram = gram + gram_ref[i].astype(F32)
    gram = resplit(gram).astype(BF16)
    for i in range(8):
        out_ref[i, ROWS:, :] = gram


def sum_kernel(in_ref, out_ref, gram_ref):
    w = in_ref[0, :ROWS, :].astype(F32)
    for i in range(1, 8):
        w = w + in_ref[i, :ROWS, :].astype(F32)
    gram_ref[...] = in_ref[:, ROWS:, :]
    mean = jnp.sum(w, axis=0, keepdims=True) * (1.0 / ROWS)
    top = jnp.max(jnp.abs(mean), axis=1, keepdims=True)
    lead = (mean / jnp.maximum(top, 1e-30)).astype(BF16)
    leadf = lead.astype(F32)
    norm = jnp.maximum(jnp.sum(leadf * leadf, axis=1, keepdims=True), 0.5)
    coef = (dot(lead, w.astype(BF16), 1, 1) / norm).astype(BF16)
    rest = w - dot(coef, lead, 0, 0)
    row = iota((TAIL, K), 0)
    wide = jnp.concatenate([coef.astype(F32), jnp.zeros((1, K - ROWS), F32)], axis=1)
    tail = jnp.where(row == 0, leadf, jnp.where(row == 1, wide, 0.0)).astype(BF16)
    body = rest.astype(BF16)
    for i in range(8):
        out_ref[i, :ROWS, :] = body
        out_ref[i, ROWS:, :] = tail


def eliminate(x):
    groups = NB // 8
    xs = [x[8 * g : 8 * g + 8] for g in range(groups)]
    sub = iota((8, 128), 0)

    def wide(a):
        return jnp.broadcast_to(a, (8, 128))

    for t in range(groups):
        at = 8 * t
        head = xs[t]
        cols = [wide(head[:, at + m : at + m + 1]) for m in range(8)]
        s = [[wide(cols[m][i : i + 1, :]) if m >= i else None for m in range(8)] for i in range(8)]
        rows = [wide(head[i : i + 1, :]) for i in range(8)]
        ratio = [[None] * 8 for _ in range(8)]
        scaled = []
        for j in range(8):
            inv = pltpu.reciprocal(s[j][j], approx=True)
            for m in range(j + 1, 8):
                ratio[j][m] = s[j][m] * inv
            for i in range(j + 1, 8):
                for m in range(i, 8):
                    s[i][m] = s[i][m] - ratio[j][i] * s[j][m]
                rows[i] = rows[i] - ratio[j][i] * rows[j]
            scaled.append(rows[j] * inv)
        for g in range(t + 1, groups):
            left, x = [], xs[g]
            for j in range(8):
                e = wide(xs[g][:, at + j : at + j + 1])
                for m in range(j):
                    e = e - ratio[m][j] * left[m]
                left.append(e)
                x = x - e * scaled[j]
            xs[g] = x
        out = rows[0] * lax.rsqrt(s[0][0])
        for j in range(1, 8):
            out = jnp.where(sub == j, rows[j] * lax.rsqrt(s[j][j]), out)
        xs[t] = out
    return jnp.concatenate(xs, axis=0)


def factor(work, blocks):
    lane = iota((NB, 128), 1)
    row = iota((NB, 128), 0)
    for b in blocks:
        at = b * NB
        base = at // 128 * 128
        x = work[at : at + NB, base : base + 128]
        if at > base:
            x = pltpu.roll(x, 128 - (at - base), 1)
        x = eliminate(jnp.where(lane < NB, x, jnp.where(lane - NB == row, 1.0, 0.0)))
        inv = pltpu.roll(x, 128 - NB, 1)[:, :NB]
        for lo, hi in ((base, K), (K, K + min(base + 128, K))):
            work[at : at + NB, lo:hi] = dot(inv, work[at : at + NB, lo:hi], 1, 0, lax.Precision.HIGHEST)
        if at + NB < K:
            down = work[at : at + NB, :K].T[at + NB :]
            for lo, hi in (((at + NB) // 128 * 128, K), (K, K + min(base + 128, K))):
                work[at + NB :, lo:hi] -= dot(down, work[at : at + NB, lo:hi], 1, 0, lax.Precision.HIGHEST)


def first_kernel(meta_ref, e0_ref, e1_ref, e2_ref, e3_ref, work):
    extra = jnp.concatenate([e[...].reshape(8 * EXTRA, K) for e in (e0_ref, e1_ref, e2_ref, e3_ref)], axis=0)
    p = iota((192, PARTS * EXTRA), 0)
    e = iota((192, PARTS * EXTRA), 1)
    slot = p // 6
    first = (((meta_ref[2] - slot // 8) & 3) * 8 + slot % 8) * EXTRA + p % 6
    pick = jnp.where((e == first) | (e == first + 6), 1.0, 0.0).astype(BF16)
    packed = dot(pick, extra, 1, 0)
    work[: K // 2, :K] = packed[: K // 2]
    work[K // 2 :, : K // 2] = packed[: K // 2, K // 2 :].T
    work[K // 2 : 3 * K // 4, K // 2 : K] = packed[K // 2 :, : K // 2]
    work[3 * K // 4 :, K // 2 : K] = packed[K // 2 :, K // 2 :]
    work[:, K:] = jnp.where(iota((K, K), 0) == iota((K, K), 1), 1.0, 0.0)
    factor(work, range(FIRST))


def rest_kernel(begun_ref, r_ref, inv_ref, work):
    work[...] = begun_ref[...]
    factor(work, range(FIRST, K // NB))
    r_ref[...] = jnp.where(iota((K, K), 0) <= iota((K, K), 1), work[:, :K], 0.0)
    inv = work[:, K:]
    high = inv.astype(BF16)
    inv_ref[:K, :] = high
    inv_ref[K:, :] = (inv - high.astype(F32)).astype(BF16)


def q_kernel(s_ref, inv_ref, q_ref):
    for k in range(4):
        a = s_ref[4 * k : 4 * k + 4].reshape(4 * TILE, K)
        rows = slice(k * 4 * TILE, (k + 1) * 4 * TILE)
        q_ref[rows, :] = (dot(a, inv_ref[:K, :], 1, 1) + dot(a, inv_ref[K:, :], 1, 1)).astype(BF16)


def solve_kernel(meta_ref, b0_ref, b1_ref, b2_ref, b3_ref, inv_ref, z_hbm, z_ref, sem):
    def solve(a):
        return dot(a, inv_ref[:K, :], 1, 1) + dot(a, inv_ref[K:, :], 1, 1)

    refs = (b0_ref, b1_ref, b2_ref, b3_ref)
    tails = jnp.concatenate([ref[:, ROWS:, :].reshape(8 * TAIL, K) for ref in refs], axis=0)
    i = iota((2 * PARTS, PARTS * TAIL), 0)
    e = iota((2 * PARTS, PARTS * TAIL), 1)
    pick = jnp.where(e == (i % PARTS) * TAIL + i // PARTS, 1.0, 0.0).astype(BF16)
    leads = dot(pick, tails, 1, 0)
    lead = solve(leads[:PARTS].astype(BF16))
    coef = leads[PARTS:, :TILE].T
    copies = []
    for k, ref in enumerate(refs):
        z = solve(ref[:, :ROWS, :].reshape(8 * ROWS, K))
        for s in range(8):
            m = 8 * k + s
            z_ref[k, s * ROWS : (s + 1) * ROWS, :] = (
                z[s * ROWS : (s + 1) * ROWS] + coef[:ROWS, m : m + 1] * lead[m : m + 1, :]
            )
        at = pl.multiple_of(((meta_ref[2] - k) & 3) * 8 * ROWS, 8 * ROWS)
        copies.append(pltpu.make_async_copy(z_ref.at[k], z_hbm.at[pl.ds(at, 8 * ROWS), :], sem.at[k]))
        copies[-1].start()
    for copy in copies:
        copy.wait()


def shape(*dims, dtype=F32):
    return jax.ShapeDtypeStruct(dims, dtype)


def cost(us):
    return pl.CostEstimate(flops=us * 10**9, bytes_accessed=2**20, transcendentals=0)


LIMIT = pltpu.CompilerParams(vmem_limit_bytes=40 * 1024 * 1024)


def on_device(tiles, block_rows, block_cols, tile_counts, omega):
    places = [lax.axis_index(axis).astype(jnp.int32).reshape(1) for axis in ("c", "y", "x")]
    meta = jnp.concatenate(places + [tile_counts[0], block_rows[0, 0], block_cols[0, 0]])
    swap = [(0, 1), (1, 0)]
    keep, send = pl.pallas_call(
        sketch_kernel,
        out_shape=(shape(HALF, K), shape(HALF, K, dtype=BF16)),
        in_specs=[SMEM] + [HBM] * 2,
        out_specs=(VMEM, VMEM),
        scratch_shapes=[
            pltpu.VMEM((RB, TILE, K), F32),
            pltpu.VMEM((SLOTS, TILE, TILE), BF16),
            pltpu.VMEM((CB, TILE, K), BF16),
            pltpu.SemaphoreType.DMA,
            pltpu.SemaphoreType.DMA((SLOTS // LOAD,)),
        ],
        compiler_params=pltpu.CompilerParams(vmem_limit_bytes=52 * 1024 * 1024),
        name="sketch",
    )(meta, tiles, omega.reshape(CB, TILE, K))

    def turn(a, k, axis="y"):
        return lax.ppermute(a, axis, [(i, (i + k) % 4) for i in range(4)])

    half = keep + lax.ppermute(send, "c", swap).astype(F32)
    quarters = half.reshape(4, PIECE, K)
    sent = [quarters[k].astype(BF16) for k in range(4)]
    sent[2], later = lax.optimization_barrier((sent[2], meta))
    order = pl.pallas_call(
        order_kernel,
        out_shape=shape(SOURCE + SLOTS, dtype=jnp.int32),
        in_specs=[SMEM],
        out_specs=SMEM,
        scratch_shapes=[pltpu.SMEM((8,), jnp.int32)],
        compiler_params=LIMIT,
        cost_estimate=cost(3),
        name="order",
    )(later)
    shard = quarters[0]
    for k in (2, 1, 3):
        shard = shard + turn(sent[k], k).astype(F32)
    shard, order = lax.optimization_barrier((shard.astype(BF16), order))
    flipped = pl.pallas_call(
        flip_kernel,
        out_shape=shape(SLOTS, TILE, TILE, dtype=BF16),
        in_specs=[SMEM, VMEM],
        out_specs=VMEM,
        compiler_params=LIMIT,
        cost_estimate=cost(3),
        name="flip",
    )(order, tiles[0, 0])
    mine = jnp.concatenate([shard] + [turn(shard, k) for k in (1, 2, 3)], axis=0)
    mine, flipped = lax.optimization_barrier((mine, flipped))
    other = lax.ppermute(mine, "c", swap)
    half_gram = pl.pallas_call(
        gram_kernel,
        out_shape=shape(K, K),
        in_specs=[VMEM],
        out_specs=VMEM,
        compiler_params=LIMIT,
        cost_estimate=cost(1),
        name="gram",
    )(mine)
    slab, *grams = pl.pallas_call(
        slab_kernel,
        out_shape=(shape(RB, TILE, K, dtype=BF16),) + (shape(8, EXTRA, K, dtype=BF16),) * 4,
        in_specs=[SMEM] + [VMEM] * 3,
        out_specs=(VMEM,) * 5,
        compiler_params=LIMIT,
        cost_estimate=cost(1),
        name="slab",
    )(meta, mine, other, half_gram)
    grams = [grams[0]] + [turn(grams[k], k, "x") for k in (1, 2, 3)]
    backs = []
    for first, last in ((1, 3), (0, 0)):
        count = last - first + 1
        backs += pl.pallas_call(
            functools.partial(back_kernel, first, last),
            out_shape=(shape(8, ROWS, K, dtype=BF16),) * count,
            in_specs=[SMEM] + [VMEM] * 2,
            out_specs=(VMEM,) * count,
            scratch_shapes=[pltpu.VMEM((4 * count, TILE, K), F32)],
            compiler_params=LIMIT,
            cost_estimate=cost(10 if first else 1),
            name=f"back{first}",
        )(order, flipped, slab)
    grams = pl.pallas_call(
        gram_sum_kernel,
        out_shape=shape(8, EXTRA, K, dtype=BF16),
        in_specs=[VMEM] * 4,
        out_specs=VMEM,
        compiler_params=LIMIT,
        name="gram_sum",
    )(*grams)
    grams, *backs[:3] = lax.optimization_barrier((grams, *backs[:3]))
    backs = [backs[3]] + [turn(backs[k - 1], k, "x") for k in (1, 2, 3)]
    grams = lax.all_to_all(grams, "z", 0, 0, tiled=True)
    size = (ROWS + EXTRA, K)
    parts = pl.pallas_call(
        partial_kernel,
        out_shape=shape(8, *size, dtype=BF16),
        in_specs=[VMEM] * 5,
        out_specs=VMEM,
        compiler_params=LIMIT,
        name="partial",
    )(*backs, grams)
    spread, gram = pl.pallas_call(
        sum_kernel,
        out_shape=(shape(8, ROWS + TAIL, K, dtype=BF16), shape(8, EXTRA, K, dtype=BF16)),
        in_specs=[VMEM],
        out_specs=(VMEM, VMEM),
        compiler_params=LIMIT,
        name="total",
    )(lax.all_to_all(parts, "z", 0, 0, tiled=True))
    extras = [gram] + [turn(gram, k, "x") for k in (1, 2, 3)]
    line = lax.all_to_all(spread, "z", 0, 0, tiled=True)
    bodies = [line] + [turn(line, k, "x") for k in (1, 2, 3)]
    begun = pl.pallas_call(
        first_kernel,
        out_shape=shape(K, 2 * K),
        in_specs=[SMEM] + [VMEM] * 4,
        out_specs=VMEM,
        compiler_params=LIMIT,
        cost_estimate=cost(3 * FIRST),
        name="first",
    )(meta, *extras)
    r, inv = pl.pallas_call(
        rest_kernel,
        out_shape=(shape(K, K), shape(2 * K, K, dtype=BF16)),
        in_specs=[VMEM],
        out_specs=(VMEM,) * 2,
        scratch_shapes=[pltpu.VMEM((K, 2 * K), F32)],
        compiler_params=LIMIT,
        cost_estimate=cost(12 - 3 * FIRST),
        name="rest",
    )(begun)
    q = pl.pallas_call(
        q_kernel,
        out_shape=shape(2 * HALF, K, dtype=BF16),
        in_specs=[VMEM] * 2,
        out_specs=VMEM,
        compiler_params=LIMIT,
        cost_estimate=cost(2),
        name="q",
    )(slab, inv)
    z = pl.pallas_call(
        solve_kernel,
        out_shape=shape(CB * TILE, K),
        in_specs=[SMEM] + [VMEM] * 5,
        out_specs=HBM,
        scratch_shapes=[pltpu.VMEM((4, 8 * ROWS, K), F32), pltpu.SemaphoreType.DMA((4,))],
        compiler_params=LIMIT,
        name="z",
    )(meta, *bodies, inv)
    return q, r, z


def solution(mesh):
    grid = Mesh(mesh.devices.reshape(8, 4, 4, 2), ("z", "x", "y", "c"))
    row, col = ("z", "x"), ("y", "c")
    placed = (
        P(row, col, None, None, None),
        P(row, col, None),
        P(row, col, None),
        P(row, col),
        P(col, None),
    )
    return jax.shard_map(
        on_device,
        mesh=grid,
        in_specs=placed,
        out_specs=(P(row, None), P(), P(col, None)),
        check_vma=False,
    )
```

```python
import functools

import jax
import jax.numpy as jnp
from jax import lax
from jax.experimental import pallas as pl
from jax.experimental.pallas import tpu as pltpu
from jax.sharding import Mesh, PartitionSpec as P

F32 = jnp.float32
BF16 = jnp.bfloat16
TILE = 128
K = 256
RB = 16
CB = 16
SLOTS = 64
HALF = RB * TILE // 2
NROW = 65536
PARTS = 32
ROWS = CB * TILE // PARTS
EXTRA = 16
TAIL = 8
GROUP = 4
NB = 64
FIRST = 1
LOAD = 8
LIVE = 3
AT = 4
COLS = AT + SLOTS
START = COLS + SLOTS
SOURCE = START + 8
PIECE = HALF // 4
VMEM = pl.BlockSpec(memory_space=pltpu.VMEM)
SMEM = pl.BlockSpec(memory_space=pltpu.SMEM)
HBM = pl.BlockSpec(memory_space=pltpu.HBM)


def dot(a, b, ca, cb, precision=None):
    return lax.dot_general(
        a, b, (((ca,), (cb,)), ((), ())), precision=precision, preferred_element_type=F32
    )


def iota(shape, dim):
    return lax.broadcasted_iota(jnp.int32, shape, dim)


def sketch_kernel(meta_ref, tiles_hbm, omega_hbm, keep_ref, send_ref, acc, tiles_ref, omega_ref, omega_sem, tile_sem):
    test = pltpu.make_async_copy(omega_hbm, omega_ref, omega_sem)
    big = [
        pltpu.make_async_copy(
            tiles_hbm.at[0, 0, pl.ds(g * LOAD, LOAD)], tiles_ref.at[pl.ds(g * LOAD, LOAD)], tile_sem.at[g]
        )
        for g in range(SLOTS // LOAD)
    ]
    big[0].start()
    test.start()
    for copy in big[1:]:
        copy.start()
    acc[...] = jnp.zeros_like(acc)
    live = meta_ref[LIVE]
    core, chip = meta_ref[0], meta_ref[1]
    test.wait()
    for g, copy in enumerate(big):
        copy.wait()

        @pl.when(g * LOAD < live)
        def _():
            prods, places = [], []
            for t in range(g * LOAD, (g + 1) * LOAD):
                prod = dot(tiles_ref[t], omega_ref[meta_ref[COLS + t] & (CB - 1)], 1, 0)
                prods.append(jnp.where(t < live, prod, 0.0))
                block = meta_ref[AT + t] & (RB - 1)
                half = (block // 8 + core) & 1
                places.append(half * 8 + ((block - 2 * chip) & 7))
            for prod, place in zip(prods, places):
                acc[place] += prod

    keep_ref[...] = acc[: RB // 2].reshape(HALF, K)
    send_ref[...] = acc[RB // 2 :].reshape(HALF, K).astype(BF16)


def order_kernel(meta_ref, sorted_ref, count):
    live = meta_ref[LIVE]
    for i in range(8):
        count[i] = 0
    for i in range(3):
        sorted_ref[i] = meta_ref[i]

    def turned(t):
        return (meta_ref[COLS + t] - 4 * meta_ref[2]) & (CB - 1)

    def chunk(t):
        return jnp.where(t < live, turned(t) // 4, 4)

    @pl.loop(0, SLOTS)
    def _(t):
        c = chunk(t)
        count[c] = count[c] + 1

    begin = jnp.int32(0)
    for i in range(5):
        here = count[i]
        sorted_ref[START + i] = begin
        count[i] = begin
        begin = begin + here

    @pl.loop(0, SLOTS)
    def _(t):
        c = chunk(t)
        at = count[c]
        count[c] = at + 1
        sorted_ref[SOURCE + at] = t
        sorted_ref[AT + at] = meta_ref[AT + t] & (RB - 1)
        sorted_ref[COLS + at] = turned(t)


def flip_kernel(meta_ref, tiles_ref, out_ref):
    @pl.loop(0, SLOTS // GROUP)
    def _(g):
        for i in range(GROUP):
            t = g * GROUP + i
            out_ref[t] = tiles_ref[meta_ref[SOURCE + t]].T


def gram_kernel(mine_ref, out_ref):
    out_ref[...] = dot(mine_ref[...], mine_ref[...], 0, 0)


def place(chunk, x):
    far = chunk ^ x
    return jnp.where(far == 3, 2, jnp.where(far == 2, 3, far))


def slab_kernel(meta_ref, mine_ref, other_ref, gram_ref, s_ref, keep_ref, give_ref):
    core, chip, x = meta_ref[0], meta_ref[1], meta_ref[2]
    for k in range(4):
        at = ((chip - k) & 3) * 2
        part = pl.ds(k * PIECE, PIECE)
        s_ref[pl.ds(core * 8 + at, 2)] = mine_ref[part, :].reshape(2, TILE, K)
        s_ref[pl.ds((1 - core) * 8 + at, 2)] = other_ref[part, :].reshape(2, TILE, K)
    gram = (gram_ref[...] + dot(other_ref[...], other_ref[...], 0, 0)) * (1.0 / NROW)
    low = gram[K // 2 :, K // 2 :]
    low = jnp.concatenate([low[: K // 4], low[K // 4 :]], axis=1)
    packed = jnp.concatenate([gram[: K // 2], low], axis=0)
    high = packed.astype(BF16)
    rest = (packed - high.astype(F32)).astype(BF16)
    e = iota((PARTS * EXTRA, 192), 0)
    p = iota((PARTS * EXTRA, 192), 1)
    slot = p // 6
    first = (place(slot // 8, x) * 8 + slot % 8) * EXTRA + p % 6
    extra = dot(jnp.where(e == first, 1.0, 0.0).astype(BF16), high, 1, 0) + dot(
        jnp.where(e == first + 6, 1.0, 0.0).astype(BF16), rest, 1, 0
    )
    extra = extra.reshape(PARTS, EXTRA, K).astype(BF16)
    keep_ref[...] = extra[: PARTS // 2]
    give_ref[...] = extra[PARTS // 2 :]


def back_kernel(first, last, meta_ref, tiles_ref, s_ref, *refs):
    *out_refs, acc = refs
    begin, end = meta_ref[START + first], meta_ref[START + last + 1]
    acc[...] = jnp.zeros_like(acc)

    @pl.loop(0, (end - begin + LOAD - 1) // LOAD)
    def _(g):
        prods, places = [], []
        for i in range(LOAD):
            t = begin + g * LOAD + i
            safe = jnp.minimum(t, SLOTS - 1)
            prod = dot(tiles_ref[safe], s_ref[meta_ref[AT + safe]], 1, 0)
            prods.append(jnp.where(t < end, prod, 0.0))
            places.append(jnp.where(t < end, meta_ref[COLS + safe] - 4 * first, 0))
        for prod, place in zip(prods, places):
            acc[place] += prod

    for k, ref in enumerate(out_refs):
        ref[...] = acc[4 * k : 4 * k + 4].reshape(8, ROWS, K).astype(BF16)


def resplit(extra):
    row = iota(extra.shape, 0) % EXTRA
    gram = extra + pltpu.roll(extra, extra.shape[0] - 6, 0)
    high = gram.astype(BF16).astype(F32)
    low = pltpu.roll(gram - high, 6, 0)
    return jnp.where(row < 6, high, jnp.where(row < 12, low, 0.0))


def gram_pair_kernel(keep_ref, got_ref, mine_ref, pass_ref):
    total = keep_ref[...].astype(F32) + got_ref[...].astype(F32)
    total = resplit(total.reshape(16 * EXTRA, K)).reshape(16, EXTRA, K).astype(BF16)
    mine_ref[...] = total[:8]
    pass_ref[...] = total[8:]


def gram_sum_kernel(mine_ref, got_ref, out_ref):
    total = mine_ref[...].astype(F32) + got_ref[...].astype(F32)
    out_ref[...] = resplit(total.reshape(8 * EXTRA, K)).reshape(8, EXTRA, K).astype(BF16)


def partial_kernel(a_ref, b_ref, c_ref, d_ref, gram_ref, out_ref):
    total = a_ref[...].astype(F32)
    for ref in (b_ref, c_ref, d_ref):
        total = total + ref[...].astype(F32)
    out_ref[:, :ROWS, :] = total.astype(BF16)
    gram = gram_ref[0].astype(F32)
    for i in range(1, 8):
        gram = gram + gram_ref[i].astype(F32)
    gram = resplit(gram).astype(BF16)
    for i in range(8):
        out_ref[i, ROWS:, :] = gram


def sum_kernel(in_ref, out_ref, gram_ref):
    w = in_ref[0, :ROWS, :].astype(F32)
    for i in range(1, 8):
        w = w + in_ref[i, :ROWS, :].astype(F32)
    gram_ref[...] = in_ref[:, ROWS:, :]
    mean = jnp.sum(w, axis=0, keepdims=True) * (1.0 / ROWS)
    top = jnp.max(jnp.abs(mean), axis=1, keepdims=True)
    lead = (mean / jnp.maximum(top, 1e-30)).astype(BF16)
    leadf = lead.astype(F32)
    norm = jnp.maximum(jnp.sum(leadf * leadf, axis=1, keepdims=True), 0.5)
    coef = (dot(lead, w.astype(BF16), 1, 1) / norm).astype(BF16)
    rest = w - dot(coef, lead, 0, 0)
    row = iota((TAIL, K), 0)
    wide = jnp.concatenate([coef.astype(F32), jnp.zeros((1, K - ROWS), F32)], axis=1)
    tail = jnp.where(row == 0, leadf, jnp.where(row == 1, wide, 0.0)).astype(BF16)
    body = rest.astype(BF16)
    for i in range(8):
        out_ref[i, :ROWS, :] = body
        out_ref[i, ROWS:, :] = tail


def eliminate(x):
    groups = NB // 8
    xs = [x[8 * g : 8 * g + 8] for g in range(groups)]
    sub = iota((8, 128), 0)

    def wide(a):
        return jnp.broadcast_to(a, (8, 128))

    for t in range(groups):
        at = 8 * t
        head = xs[t]
        cols = [wide(head[:, at + m : at + m + 1]) for m in range(8)]
        s = [[wide(cols[m][i : i + 1, :]) if m >= i else None for m in range(8)] for i in range(8)]
        rows = [wide(head[i : i + 1, :]) for i in range(8)]
        ratio = [[None] * 8 for _ in range(8)]
        scaled = []
        for j in range(8):
            inv = pltpu.reciprocal(s[j][j], approx=True)
            for m in range(j + 1, 8):
                ratio[j][m] = s[j][m] * inv
            for i in range(j + 1, 8):
                for m in range(i, 8):
                    s[i][m] = s[i][m] - ratio[j][i] * s[j][m]
                rows[i] = rows[i] - ratio[j][i] * rows[j]
            scaled.append(rows[j] * inv)
        for g in range(t + 1, groups):
            left, x = [], xs[g]
            for j in range(8):
                e = wide(xs[g][:, at + j : at + j + 1])
                for m in range(j):
                    e = e - ratio[m][j] * left[m]
                left.append(e)
                x = x - e * scaled[j]
            xs[g] = x
        out = rows[0] * lax.rsqrt(s[0][0])
        for j in range(1, 8):
            out = jnp.where(sub == j, rows[j] * lax.rsqrt(s[j][j]), out)
        xs[t] = out
    return jnp.concatenate(xs, axis=0)


def factor(work, blocks):
    lane = iota((NB, 128), 1)
    row = iota((NB, 128), 0)
    for b in blocks:
        at = b * NB
        base = at // 128 * 128
        x = work[at : at + NB, base : base + 128]
        if at > base:
            x = pltpu.roll(x, 128 - (at - base), 1)
        x = eliminate(jnp.where(lane < NB, x, jnp.where(lane - NB == row, 1.0, 0.0)))
        inv = pltpu.roll(x, 128 - NB, 1)[:, :NB]
        for lo, hi in ((base, K), (K, K + min(base + 128, K))):
            work[at : at + NB, lo:hi] = dot(inv, work[at : at + NB, lo:hi], 1, 0, lax.Precision.HIGHEST)
        if at + NB < K:
            down = work[at : at + NB, :K].T[at + NB :]
            for lo, hi in (((at + NB) // 128 * 128, K), (K, K + min(base + 128, K))):
                work[at + NB :, lo:hi] -= dot(down, work[at : at + NB, lo:hi], 1, 0, lax.Precision.HIGHEST)


def first_kernel(meta_ref, e0_ref, e1_ref, e2_ref, work):
    extra = jnp.concatenate([e[...].reshape(-1, K) for e in (e0_ref, e1_ref, e2_ref)], axis=0)
    p = iota((192, PARTS * EXTRA), 0)
    e = iota((192, PARTS * EXTRA), 1)
    slot = p // 6
    first = (place(slot // 8, meta_ref[2]) * 8 + slot % 8) * EXTRA + p % 6
    pick = jnp.where((e == first) | (e == first + 6), 1.0, 0.0).astype(BF16)
    packed = dot(pick, extra, 1, 0)
    work[: K // 2, :K] = packed[: K // 2]
    work[K // 2 :, : K // 2] = packed[: K // 2, K // 2 :].T
    work[K // 2 : 3 * K // 4, K // 2 : K] = packed[K // 2 :, : K // 2]
    work[3 * K // 4 :, K // 2 : K] = packed[K // 2 :, K // 2 :]
    work[:, K:] = jnp.where(iota((K, K), 0) == iota((K, K), 1), 1.0, 0.0)
    factor(work, range(FIRST))


def rest_kernel(begun_ref, r_ref, inv_ref, work):
    work[...] = begun_ref[...]
    factor(work, range(FIRST, K // NB))
    r_ref[...] = jnp.where(iota((K, K), 0) <= iota((K, K), 1), work[:, :K], 0.0)
    inv = work[:, K:]
    high = inv.astype(BF16)
    inv_ref[:K, :] = high
    inv_ref[K:, :] = (inv - high.astype(F32)).astype(BF16)


def q_kernel(s_ref, inv_ref, q_ref):
    for k in range(4):
        a = s_ref[4 * k : 4 * k + 4].reshape(4 * TILE, K)
        rows = slice(k * 4 * TILE, (k + 1) * 4 * TILE)
        q_ref[rows, :] = (dot(a, inv_ref[:K, :], 1, 1) + dot(a, inv_ref[K:, :], 1, 1)).astype(BF16)


def solve_kernel(meta_ref, b0_ref, b1_ref, b2_ref, b3_ref, inv_ref, z_hbm, z_ref, sem):
    def solve(a):
        return dot(a, inv_ref[:K, :], 1, 1) + dot(a, inv_ref[K:, :], 1, 1)

    refs = (b0_ref, b1_ref, b2_ref, b3_ref)
    tails = jnp.concatenate([ref[:, ROWS:, :].reshape(8 * TAIL, K) for ref in refs], axis=0)
    i = iota((2 * PARTS, PARTS * TAIL), 0)
    e = iota((2 * PARTS, PARTS * TAIL), 1)
    pick = jnp.where(e == (i % PARTS) * TAIL + i // PARTS, 1.0, 0.0).astype(BF16)
    leads = dot(pick, tails, 1, 0)
    lead = solve(leads[:PARTS].astype(BF16))
    coef = leads[PARTS:, :TILE].T
    copies = []
    for k, ref in enumerate(refs):
        z = solve(ref[:, :ROWS, :].reshape(8 * ROWS, K))
        for s in range(8):
            m = 8 * k + s
            z_ref[k, s * ROWS : (s + 1) * ROWS, :] = (
                z[s * ROWS : (s + 1) * ROWS] + coef[:ROWS, m : m + 1] * lead[m : m + 1, :]
            )
        at = pl.multiple_of(((meta_ref[2] - k) & 3) * 8 * ROWS, 8 * ROWS)
        copies.append(pltpu.make_async_copy(z_ref.at[k], z_hbm.at[pl.ds(at, 8 * ROWS), :], sem.at[k]))
        copies[-1].start()
    for copy in copies:
        copy.wait()


def shape(*dims, dtype=F32):
    return jax.ShapeDtypeStruct(dims, dtype)


def cost(us):
    return pl.CostEstimate(flops=us * 10**9, bytes_accessed=2**20, transcendentals=0)


LIMIT = pltpu.CompilerParams(vmem_limit_bytes=40 * 1024 * 1024)


def on_device(tiles, block_rows, block_cols, tile_counts, omega):
    places = [lax.axis_index(axis).astype(jnp.int32).reshape(1) for axis in ("c", "y", "x")]
    meta = jnp.concatenate(places + [tile_counts[0], block_rows[0, 0], block_cols[0, 0]])
    swap = [(0, 1), (1, 0)]
    keep, send = pl.pallas_call(
        sketch_kernel,
        out_shape=(shape(HALF, K), shape(HALF, K, dtype=BF16)),
        in_specs=[SMEM] + [HBM] * 2,
        out_specs=(VMEM, VMEM),
        scratch_shapes=[
            pltpu.VMEM((RB, TILE, K), F32),
            pltpu.VMEM((SLOTS, TILE, TILE), BF16),
            pltpu.VMEM((CB, TILE, K), BF16),
            pltpu.SemaphoreType.DMA,
            pltpu.SemaphoreType.DMA((SLOTS // LOAD,)),
        ],
        compiler_params=pltpu.CompilerParams(vmem_limit_bytes=52 * 1024 * 1024),
        name="sketch",
    )(meta, tiles, omega.reshape(CB, TILE, K))

    def turn(a, k, axis="y"):
        return lax.ppermute(a, axis, [(i, (i + k) % 4) for i in range(4)])

    half = keep + lax.ppermute(send, "c", swap).astype(F32)
    quarters = half.reshape(4, PIECE, K)
    sent = [quarters[k].astype(BF16) for k in range(4)]
    sent[2], later = lax.optimization_barrier((sent[2], meta))
    order = pl.pallas_call(
        order_kernel,
        out_shape=shape(SOURCE + SLOTS, dtype=jnp.int32),
        in_specs=[SMEM],
        out_specs=SMEM,
        scratch_shapes=[pltpu.SMEM((8,), jnp.int32)],
        compiler_params=LIMIT,
        cost_estimate=cost(3),
        name="order",
    )(later)
    shard = quarters[0]
    for k in (2, 1, 3):
        shard = shard + turn(sent[k], k).astype(F32)
    shard, order = lax.optimization_barrier((shard.astype(BF16), order))
    flipped = pl.pallas_call(
        flip_kernel,
        out_shape=shape(SLOTS, TILE, TILE, dtype=BF16),
        in_specs=[SMEM, VMEM],
        out_specs=VMEM,
        compiler_params=LIMIT,
        cost_estimate=cost(3),
        name="flip",
    )(order, tiles[0, 0])
    mine = jnp.concatenate([shard] + [turn(shard, k) for k in (1, 2, 3)], axis=0)
    mine, flipped = lax.optimization_barrier((mine, flipped))
    other = lax.ppermute(mine, "c", swap)
    half_gram = pl.pallas_call(
        gram_kernel,
        out_shape=shape(K, K),
        in_specs=[VMEM],
        out_specs=VMEM,
        compiler_params=LIMIT,
        cost_estimate=cost(1),
        name="gram",
    )(mine)
    slab, keep, give = pl.pallas_call(
        slab_kernel,
        out_shape=(shape(RB, TILE, K, dtype=BF16),) + (shape(16, EXTRA, K, dtype=BF16),) * 2,
        in_specs=[SMEM] + [VMEM] * 3,
        out_specs=(VMEM,) * 3,
        compiler_params=LIMIT,
        cost_estimate=cost(1),
        name="slab",
    )(meta, mine, other, half_gram)

    def mirror(a, bits):
        return lax.ppermute(a, "x", [(i, i ^ bits) for i in range(4)])

    got = mirror(give, 3)
    backs = []
    for first, last in ((1, 3), (0, 0)):
        count = last - first + 1
        backs += pl.pallas_call(
            functools.partial(back_kernel, first, last),
            out_shape=(shape(8, ROWS, K, dtype=BF16),) * count,
            in_specs=[SMEM] + [VMEM] * 2,
            out_specs=(VMEM,) * count,
            scratch_shapes=[pltpu.VMEM((4 * count, TILE, K), F32)],
            compiler_params=LIMIT,
            cost_estimate=cost(10 if first else 1),
            name=f"back{first}",
        )(order, flipped, slab)
    got, *backs[:3] = lax.optimization_barrier((got, *backs[:3]))
    own, away = pl.pallas_call(
        gram_pair_kernel,
        out_shape=(shape(8, EXTRA, K, dtype=BF16),) * 2,
        in_specs=[VMEM] * 2,
        out_specs=(VMEM,) * 2,
        compiler_params=LIMIT,
        name="gram_pair",
    )(keep, got)
    away = mirror(away, 1)
    away, backs[3] = lax.optimization_barrier((away, backs[3]))
    grams = pl.pallas_call(
        gram_sum_kernel,
        out_shape=shape(8, EXTRA, K, dtype=BF16),
        in_specs=[VMEM] * 2,
        out_specs=VMEM,
        compiler_params=LIMIT,
        name="gram_sum",
    )(own, away)
    grams, *backs[:3] = lax.optimization_barrier((grams, *backs[:3]))
    backs = [backs[3]] + [turn(backs[k - 1], k, "x") for k in (1, 2, 3)]
    grams = lax.all_to_all(grams, "z", 0, 0, tiled=True)
    size = (ROWS + EXTRA, K)
    parts = pl.pallas_call(
        partial_kernel,
        out_shape=shape(8, *size, dtype=BF16),
        in_specs=[VMEM] * 5,
        out_specs=VMEM,
        compiler_params=LIMIT,
        name="partial",
    )(*backs, grams)
    spread, gram = pl.pallas_call(
        sum_kernel,
        out_shape=(shape(8, ROWS + TAIL, K, dtype=BF16), shape(8, EXTRA, K, dtype=BF16)),
        in_specs=[VMEM],
        out_specs=(VMEM, VMEM),
        compiler_params=LIMIT,
        name="total",
    )(lax.all_to_all(parts, "z", 0, 0, tiled=True))
    near = mirror(gram, 1)
    extras = [gram, near, mirror(jnp.concatenate([gram, near], axis=0), 3)]
    line = lax.all_to_all(spread, "z", 0, 0, tiled=True)
    bodies = [line] + [turn(line, k, "x") for k in (1, 2, 3)]
    begun = pl.pallas_call(
        first_kernel,
        out_shape=shape(K, 2 * K),
        in_specs=[SMEM] + [VMEM] * 3,
        out_specs=VMEM,
        compiler_params=LIMIT,
        cost_estimate=cost(3 * FIRST),
        name="first",
    )(meta, *extras)
    r, inv = pl.pallas_call(
        rest_kernel,
        out_shape=(shape(K, K), shape(2 * K, K, dtype=BF16)),
        in_specs=[VMEM],
        out_specs=(VMEM,) * 2,
        scratch_shapes=[pltpu.VMEM((K, 2 * K), F32)],
        compiler_params=LIMIT,
        cost_estimate=cost(12 - 3 * FIRST),
        name="rest",
    )(begun)
    q = pl.pallas_call(
        q_kernel,
        out_shape=shape(2 * HALF, K, dtype=BF16),
        in_specs=[VMEM] * 2,
        out_specs=VMEM,
        compiler_params=LIMIT,
        cost_estimate=cost(2),
        name="q",
    )(slab, inv)
    z = pl.pallas_call(
        solve_kernel,
        out_shape=shape(CB * TILE, K),
        in_specs=[SMEM] + [VMEM] * 5,
        out_specs=HBM,
        scratch_shapes=[pltpu.VMEM((4, 8 * ROWS, K), F32), pltpu.SemaphoreType.DMA((4,))],
        compiler_params=LIMIT,
        name="z",
    )(meta, *bodies, inv)
    return q, r, z


def solution(mesh):
    grid = Mesh(mesh.devices.reshape(8, 4, 4, 2), ("z", "x", "y", "c"))
    row, col = ("z", "x"), ("y", "c")
    placed = (
        P(row, col, None, None, None),
        P(row, col, None),
        P(row, col, None),
        P(row, col),
        P(col, None),
    )
    return jax.shard_map(
        on_device,
        mesh=grid,
        in_specs=placed,
        out_specs=(P(row, None), P(), P(col, None)),
        check_vma=False,
    )
```

```python
import functools

import jax
import jax.numpy as jnp
from jax import lax
from jax.experimental import pallas as pl
from jax.experimental.pallas import tpu as pltpu
from jax.sharding import Mesh, PartitionSpec as P

F32 = jnp.float32
BF16 = jnp.bfloat16
TILE = 128
K = 256
RB = 16
CB = 16
SLOTS = 64
HALF = RB * TILE // 2
NROW = 65536
PARTS = 32
ROWS = CB * TILE // PARTS
EXTRA = 16
TAIL = 8
GROUP = 4
NB = 64
FIRST = 1
LOAD = 8
FETCH = 16
LIVE = 3
AT = 4
COLS = AT + SLOTS
START = COLS + SLOTS
SOURCE = START + 8
PIECE = HALF // 4
VMEM = pl.BlockSpec(memory_space=pltpu.VMEM)
SMEM = pl.BlockSpec(memory_space=pltpu.SMEM)
HBM = pl.BlockSpec(memory_space=pltpu.HBM)


def dot(a, b, ca, cb, precision=None):
    return lax.dot_general(
        a, b, (((ca,), (cb,)), ((), ())), precision=precision, preferred_element_type=F32
    )


def iota(shape, dim):
    return lax.broadcasted_iota(jnp.int32, shape, dim)


def sketch_kernel(meta_ref, tiles_hbm, omega_hbm, keep_ref, send_ref, acc, tiles_ref, omega_ref, omega_sem, tile_sem):
    test = pltpu.make_async_copy(omega_hbm, omega_ref, omega_sem)
    big = [
        pltpu.make_async_copy(
            tiles_hbm.at[0, 0, pl.ds(g * FETCH, FETCH)], tiles_ref.at[pl.ds(g * FETCH, FETCH)], tile_sem.at[g]
        )
        for g in range(SLOTS // FETCH)
    ]
    big[0].start()
    test.start()
    for copy in big[1:]:
        copy.start()
    acc[...] = jnp.zeros_like(acc)
    live = meta_ref[LIVE]
    core, chip = meta_ref[0], meta_ref[1]
    test.wait()
    for g, copy in enumerate(big):
        copy.wait()

        @pl.when(g * FETCH < live)
        def _():
            prods, places = [], []
            for t in range(g * FETCH, (g + 1) * FETCH):
                prod = dot(tiles_ref[t], omega_ref[meta_ref[COLS + t] & (CB - 1)], 1, 0)
                prods.append(jnp.where(t < live, prod, 0.0))
                block = meta_ref[AT + t] & (RB - 1)
                half = (block // 8 + core) & 1
                places.append(half * 8 + ((block - 2 * chip) & 7))
            for prod, place in zip(prods, places):
                acc[place] += prod

    keep_ref[...] = acc[: RB // 2].reshape(HALF, K)
    send_ref[...] = acc[RB // 2 :].reshape(HALF, K).astype(BF16)


def order_kernel(meta_ref, sorted_ref, count):
    live = meta_ref[LIVE]
    for i in range(8):
        count[i] = 0
    for i in range(3):
        sorted_ref[i] = meta_ref[i]

    def turned(t):
        return (meta_ref[COLS + t] - 4 * meta_ref[2]) & (CB - 1)

    def chunk(t):
        return jnp.where(t < live, turned(t) // 4, 4)

    @pl.loop(0, SLOTS)
    def _(t):
        c = chunk(t)
        count[c] = count[c] + 1

    begin = jnp.int32(0)
    for i in range(5):
        here = count[i]
        sorted_ref[START + i] = begin
        count[i] = begin
        begin = begin + here

    @pl.loop(0, SLOTS)
    def _(t):
        c = chunk(t)
        at = count[c]
        count[c] = at + 1
        sorted_ref[SOURCE + at] = t
        sorted_ref[AT + at] = meta_ref[AT + t] & (RB - 1)
        sorted_ref[COLS + at] = turned(t)


def flip_kernel(meta_ref, tiles_ref, out_ref):
    @pl.loop(0, SLOTS // GROUP)
    def _(g):
        for i in range(GROUP):
            t = g * GROUP + i
            out_ref[t] = tiles_ref[meta_ref[SOURCE + t]].T


def gram_kernel(mine_ref, out_ref):
    out_ref[...] = dot(mine_ref[...], mine_ref[...], 0, 0)


def place(chunk, x):
    far = chunk ^ x
    return jnp.where(far == 3, 2, jnp.where(far == 2, 3, far))


def slab_kernel(meta_ref, mine_ref, other_ref, gram_ref, s_ref, keep_ref, give_ref):
    core, chip, x = meta_ref[0], meta_ref[1], meta_ref[2]
    for k in range(4):
        at = ((chip - k) & 3) * 2
        part = pl.ds(k * PIECE, PIECE)
        s_ref[pl.ds(core * 8 + at, 2)] = mine_ref[part, :].reshape(2, TILE, K)
        s_ref[pl.ds((1 - core) * 8 + at, 2)] = other_ref[part, :].reshape(2, TILE, K)
    gram = (gram_ref[...] + dot(other_ref[...], other_ref[...], 0, 0)) * (1.0 / NROW)
    low = gram[K // 2 :, K // 2 :]
    low = jnp.concatenate([low[: K // 4], low[K // 4 :]], axis=1)
    packed = jnp.concatenate([gram[: K // 2], low], axis=0)
    high = packed.astype(BF16)
    rest = (packed - high.astype(F32)).astype(BF16)
    e = iota((PARTS * EXTRA, 192), 0)
    p = iota((PARTS * EXTRA, 192), 1)
    slot = p // 6
    first = (place(slot // 8, x) * 8 + slot % 8) * EXTRA + p % 6
    extra = dot(jnp.where(e == first, 1.0, 0.0).astype(BF16), high, 1, 0) + dot(
        jnp.where(e == first + 6, 1.0, 0.0).astype(BF16), rest, 1, 0
    )
    extra = extra.reshape(PARTS, EXTRA, K).astype(BF16)
    keep_ref[...] = extra[: PARTS // 2]
    give_ref[...] = extra[PARTS // 2 :]


def back_kernel(first, last, meta_ref, tiles_ref, s_ref, *refs):
    *out_refs, acc = refs
    begin, end = meta_ref[START + first], meta_ref[START + last + 1]
    acc[...] = jnp.zeros_like(acc)

    @pl.loop(0, (end - begin + LOAD - 1) // LOAD)
    def _(g):
        prods, places = [], []
        for i in range(LOAD):
            t = begin + g * LOAD + i
            safe = jnp.minimum(t, SLOTS - 1)
            prod = dot(tiles_ref[safe], s_ref[meta_ref[AT + safe]], 1, 0)
            prods.append(jnp.where(t < end, prod, 0.0))
            places.append(jnp.where(t < end, meta_ref[COLS + safe] - 4 * first, 0))
        for prod, place in zip(prods, places):
            acc[place] += prod

    for k, ref in enumerate(out_refs):
        ref[...] = acc[4 * k : 4 * k + 4].reshape(8, ROWS, K).astype(BF16)


def resplit(extra):
    row = iota(extra.shape, 0) % EXTRA
    gram = extra + pltpu.roll(extra, extra.shape[0] - 6, 0)
    high = gram.astype(BF16).astype(F32)
    low = pltpu.roll(gram - high, 6, 0)
    return jnp.where(row < 6, high, jnp.where(row < 12, low, 0.0))


def gram_pair_kernel(keep_ref, got_ref, mine_ref, pass_ref):
    total = keep_ref[...].astype(F32) + got_ref[...].astype(F32)
    total = resplit(total.reshape(16 * EXTRA, K)).reshape(16, EXTRA, K).astype(BF16)
    mine_ref[...] = total[:8]
    pass_ref[...] = total[8:]


def gram_sum_kernel(mine_ref, got_ref, out_ref):
    total = mine_ref[...].astype(F32) + got_ref[...].astype(F32)
    out_ref[...] = resplit(total.reshape(8 * EXTRA, K)).reshape(8, EXTRA, K).astype(BF16)


def partial_kernel(a_ref, b_ref, c_ref, d_ref, gram_ref, out_ref):
    total = a_ref[...].astype(F32)
    for ref in (b_ref, c_ref, d_ref):
        total = total + ref[...].astype(F32)
    out_ref[:, :ROWS, :] = total.astype(BF16)
    gram = gram_ref[0].astype(F32)
    for i in range(1, 8):
        gram = gram + gram_ref[i].astype(F32)
    gram = resplit(gram).astype(BF16)
    for i in range(8):
        out_ref[i, ROWS:, :] = gram


def sum_kernel(in_ref, out_ref, gram_ref):
    w = in_ref[0, :ROWS, :].astype(F32)
    for i in range(1, 8):
        w = w + in_ref[i, :ROWS, :].astype(F32)
    gram_ref[...] = in_ref[:, ROWS:, :]
    mean = jnp.sum(w, axis=0, keepdims=True) * (1.0 / ROWS)
    top = jnp.max(jnp.abs(mean), axis=1, keepdims=True)
    lead = (mean / jnp.maximum(top, 1e-30)).astype(BF16)
    leadf = lead.astype(F32)
    norm = jnp.maximum(jnp.sum(leadf * leadf, axis=1, keepdims=True), 0.5)
    coef = (dot(lead, w.astype(BF16), 1, 1) / norm).astype(BF16)
    rest = w - dot(coef, lead, 0, 0)
    row = iota((TAIL, K), 0)
    wide = jnp.concatenate([coef.astype(F32), jnp.zeros((1, K - ROWS), F32)], axis=1)
    tail = jnp.where(row == 0, leadf, jnp.where(row == 1, wide, 0.0)).astype(BF16)
    body = rest.astype(BF16)
    for i in range(8):
        out_ref[i, :ROWS, :] = body
        out_ref[i, ROWS:, :] = tail


def eliminate(x):
    groups = NB // 8
    xs = [x[8 * g : 8 * g + 8] for g in range(groups)]
    sub = iota((8, 128), 0)

    def wide(a):
        return jnp.broadcast_to(a, (8, 128))

    for t in range(groups):
        at = 8 * t
        head = xs[t]
        cols = [wide(head[:, at + m : at + m + 1]) for m in range(8)]
        s = [[wide(cols[m][i : i + 1, :]) if m >= i else None for m in range(8)] for i in range(8)]
        rows = [wide(head[i : i + 1, :]) for i in range(8)]
        ratio = [[None] * 8 for _ in range(8)]
        scaled = []
        for j in range(8):
            inv = pltpu.reciprocal(s[j][j], approx=True)
            for m in range(j + 1, 8):
                ratio[j][m] = s[j][m] * inv
            for i in range(j + 1, 8):
                for m in range(i, 8):
                    s[i][m] = s[i][m] - ratio[j][i] * s[j][m]
                rows[i] = rows[i] - ratio[j][i] * rows[j]
            scaled.append(rows[j] * inv)
        for g in range(t + 1, groups):
            left, x = [], xs[g]
            for j in range(8):
                e = wide(xs[g][:, at + j : at + j + 1])
                for m in range(j):
                    e = e - ratio[m][j] * left[m]
                left.append(e)
                x = x - e * scaled[j]
            xs[g] = x
        out = rows[0] * lax.rsqrt(s[0][0])
        for j in range(1, 8):
            out = jnp.where(sub == j, rows[j] * lax.rsqrt(s[j][j]), out)
        xs[t] = out
    return jnp.concatenate(xs, axis=0)


def factor(work, blocks):
    lane = iota((NB, 128), 1)
    row = iota((NB, 128), 0)
    for b in blocks:
        at = b * NB
        base = at // 128 * 128
        x = work[at : at + NB, base : base + 128]
        if at > base:
            x = pltpu.roll(x, 128 - (at - base), 1)
        x = eliminate(jnp.where(lane < NB, x, jnp.where(lane - NB == row, 1.0, 0.0)))
        inv = pltpu.roll(x, 128 - NB, 1)[:, :NB]
        for lo, hi in ((base, K), (K, K + min(base + 128, K))):
            work[at : at + NB, lo:hi] = dot(inv, work[at : at + NB, lo:hi], 1, 0, lax.Precision.HIGHEST)
        if at + NB < K:
            down = work[at : at + NB, :K].T[at + NB :]
            for lo, hi in (((at + NB) // 128 * 128, K), (K, K + min(base + 128, K))):
                work[at + NB :, lo:hi] -= dot(down, work[at : at + NB, lo:hi], 1, 0, lax.Precision.HIGHEST)


def first_kernel(meta_ref, e0_ref, e1_ref, e2_ref, work):
    extra = jnp.concatenate([e[...].reshape(-1, K) for e in (e0_ref, e1_ref, e2_ref)], axis=0)
    p = iota((192, PARTS * EXTRA), 0)
    e = iota((192, PARTS * EXTRA), 1)
    slot = p // 6
    first = (place(slot // 8, meta_ref[2]) * 8 + slot % 8) * EXTRA + p % 6
    pick = jnp.where((e == first) | (e == first + 6), 1.0, 0.0).astype(BF16)
    packed = dot(pick, extra, 1, 0)
    work[: K // 2, :K] = packed[: K // 2]
    work[K // 2 :, : K // 2] = packed[: K // 2, K // 2 :].T
    work[K // 2 : 3 * K // 4, K // 2 : K] = packed[K // 2 :, : K // 2]
    work[3 * K // 4 :, K // 2 : K] = packed[K // 2 :, K // 2 :]
    work[:, K:] = jnp.where(iota((K, K), 0) == iota((K, K), 1), 1.0, 0.0)
    factor(work, range(FIRST))


def rest_kernel(begun_ref, r_ref, inv_ref, work):
    work[...] = begun_ref[...]
    factor(work, range(FIRST, K // NB))
    r_ref[...] = jnp.where(iota((K, K), 0) <= iota((K, K), 1), work[:, :K], 0.0)
    inv = work[:, K:]
    high = inv.astype(BF16)
    inv_ref[:K, :] = high
    inv_ref[K:, :] = (inv - high.astype(F32)).astype(BF16)


def q_kernel(s_ref, inv_ref, q_ref):
    for k in range(4):
        a = s_ref[4 * k : 4 * k + 4].reshape(4 * TILE, K)
        rows = slice(k * 4 * TILE, (k + 1) * 4 * TILE)
        q_ref[rows, :] = (dot(a, inv_ref[:K, :], 1, 1) + dot(a, inv_ref[K:, :], 1, 1)).astype(BF16)


def solve_kernel(meta_ref, b0_ref, b1_ref, b2_ref, b3_ref, inv_ref, z_hbm, z_ref, sem):
    def solve(a):
        return dot(a, inv_ref[:K, :], 1, 1) + dot(a, inv_ref[K:, :], 1, 1)

    refs = (b0_ref, b1_ref, b2_ref, b3_ref)
    tails = jnp.concatenate([ref[:, ROWS:, :].reshape(8 * TAIL, K) for ref in refs], axis=0)
    i = iota((2 * PARTS, PARTS * TAIL), 0)
    e = iota((2 * PARTS, PARTS * TAIL), 1)
    pick = jnp.where(e == (i % PARTS) * TAIL + i // PARTS, 1.0, 0.0).astype(BF16)
    leads = dot(pick, tails, 1, 0)
    lead = solve(leads[:PARTS].astype(BF16))
    coef = leads[PARTS:, :TILE].T
    copies = []
    for k, ref in enumerate(refs):
        z = solve(ref[:, :ROWS, :].reshape(8 * ROWS, K))
        for s in range(8):
            m = 8 * k + s
            z_ref[k, s * ROWS : (s + 1) * ROWS, :] = (
                z[s * ROWS : (s + 1) * ROWS] + coef[:ROWS, m : m + 1] * lead[m : m + 1, :]
            )
        at = pl.multiple_of(((meta_ref[2] - k) & 3) * 8 * ROWS, 8 * ROWS)
        copies.append(pltpu.make_async_copy(z_ref.at[k], z_hbm.at[pl.ds(at, 8 * ROWS), :], sem.at[k]))
        copies[-1].start()
    for copy in copies:
        copy.wait()


def shape(*dims, dtype=F32):
    return jax.ShapeDtypeStruct(dims, dtype)


def cost(us):
    return pl.CostEstimate(flops=us * 10**9, bytes_accessed=2**20, transcendentals=0)


LIMIT = pltpu.CompilerParams(vmem_limit_bytes=40 * 1024 * 1024)


def on_device(tiles, block_rows, block_cols, tile_counts, omega):
    places = [lax.axis_index(axis).astype(jnp.int32).reshape(1) for axis in ("c", "y", "x")]
    meta = jnp.concatenate(places + [tile_counts[0], block_rows[0, 0], block_cols[0, 0]])
    swap = [(0, 1), (1, 0)]
    keep, send = pl.pallas_call(
        sketch_kernel,
        out_shape=(shape(HALF, K), shape(HALF, K, dtype=BF16)),
        in_specs=[SMEM] + [HBM] * 2,
        out_specs=(VMEM, VMEM),
        scratch_shapes=[
            pltpu.VMEM((RB, TILE, K), F32),
            pltpu.VMEM((SLOTS, TILE, TILE), BF16),
            pltpu.VMEM((CB, TILE, K), BF16),
            pltpu.SemaphoreType.DMA,
            pltpu.SemaphoreType.DMA((SLOTS // FETCH,)),
        ],
        compiler_params=pltpu.CompilerParams(vmem_limit_bytes=52 * 1024 * 1024),
        name="sketch",
    )(meta, tiles, omega.reshape(CB, TILE, K))

    def turn(a, k, axis="y"):
        return lax.ppermute(a, axis, [(i, (i + k) % 4) for i in range(4)])

    half = keep + lax.ppermute(send, "c", swap).astype(F32)
    quarters = half.reshape(4, PIECE, K)
    sent = [quarters[k].astype(BF16) for k in range(4)]
    sent[2], later = lax.optimization_barrier((sent[2], meta))
    order = pl.pallas_call(
        order_kernel,
        out_shape=shape(SOURCE + SLOTS, dtype=jnp.int32),
        in_specs=[SMEM],
        out_specs=SMEM,
        scratch_shapes=[pltpu.SMEM((8,), jnp.int32)],
        compiler_params=LIMIT,
        cost_estimate=cost(3),
        name="order",
    )(later)
    shard = quarters[0]
    for k in (2, 1, 3):
        shard = shard + turn(sent[k], k).astype(F32)
    shard, order = lax.optimization_barrier((shard.astype(BF16), order))
    flipped = pl.pallas_call(
        flip_kernel,
        out_shape=shape(SLOTS, TILE, TILE, dtype=BF16),
        in_specs=[SMEM, VMEM],
        out_specs=VMEM,
        compiler_params=LIMIT,
        cost_estimate=cost(3),
        name="flip",
    )(order, tiles[0, 0])
    mine = jnp.concatenate([shard] + [turn(shard, k) for k in (1, 2, 3)], axis=0)
    mine, flipped = lax.optimization_barrier((mine, flipped))
    other = lax.ppermute(mine, "c", swap)
    half_gram = pl.pallas_call(
        gram_kernel,
        out_shape=shape(K, K),
        in_specs=[VMEM],
        out_specs=VMEM,
        compiler_params=LIMIT,
        cost_estimate=cost(1),
        name="gram",
    )(mine)
    slab, keep, give = pl.pallas_call(
        slab_kernel,
        out_shape=(shape(RB, TILE, K, dtype=BF16),) + (shape(16, EXTRA, K, dtype=BF16),) * 2,
        in_specs=[SMEM] + [VMEM] * 3,
        out_specs=(VMEM,) * 3,
        compiler_params=LIMIT,
        cost_estimate=cost(1),
        name="slab",
    )(meta, mine, other, half_gram)

    def mirror(a, bits):
        return lax.ppermute(a, "x", [(i, i ^ bits) for i in range(4)])

    got = mirror(give, 3)
    backs = []
    for first, last in ((1, 3), (0, 0)):
        count = last - first + 1
        backs += pl.pallas_call(
            functools.partial(back_kernel, first, last),
            out_shape=(shape(8, ROWS, K, dtype=BF16),) * count,
            in_specs=[SMEM] + [VMEM] * 2,
            out_specs=(VMEM,) * count,
            scratch_shapes=[pltpu.VMEM((4 * count, TILE, K), F32)],
            compiler_params=LIMIT,
            cost_estimate=cost(10 if first else 1),
            name=f"back{first}",
        )(order, flipped, slab)
    got, *backs[:3] = lax.optimization_barrier((got, *backs[:3]))
    own, away = pl.pallas_call(
        gram_pair_kernel,
        out_shape=(shape(8, EXTRA, K, dtype=BF16),) * 2,
        in_specs=[VMEM] * 2,
        out_specs=(VMEM,) * 2,
        compiler_params=LIMIT,
        name="gram_pair",
    )(keep, got)
    away = mirror(away, 1)
    away, backs[3] = lax.optimization_barrier((away, backs[3]))
    grams = pl.pallas_call(
        gram_sum_kernel,
        out_shape=shape(8, EXTRA, K, dtype=BF16),
        in_specs=[VMEM] * 2,
        out_specs=VMEM,
        compiler_params=LIMIT,
        name="gram_sum",
    )(own, away)
    grams, *backs[:3] = lax.optimization_barrier((grams, *backs[:3]))
    backs = [backs[3]] + [turn(backs[k - 1], k, "x") for k in (1, 2, 3)]
    grams = lax.all_to_all(grams, "z", 0, 0, tiled=True)
    size = (ROWS + EXTRA, K)
    parts = pl.pallas_call(
        partial_kernel,
        out_shape=shape(8, *size, dtype=BF16),
        in_specs=[VMEM] * 5,
        out_specs=VMEM,
        compiler_params=LIMIT,
        name="partial",
    )(*backs, grams)
    spread, gram = pl.pallas_call(
        sum_kernel,
        out_shape=(shape(8, ROWS + TAIL, K, dtype=BF16), shape(8, EXTRA, K, dtype=BF16)),
        in_specs=[VMEM],
        out_specs=(VMEM, VMEM),
        compiler_params=LIMIT,
        name="total",
    )(lax.all_to_all(parts, "z", 0, 0, tiled=True))
    near = mirror(gram, 1)
    extras = [gram, near, mirror(jnp.concatenate([gram, near], axis=0), 3)]
    line = lax.all_to_all(spread, "z", 0, 0, tiled=True)
    bodies = [line] + [turn(line, k, "x") for k in (1, 2, 3)]
    begun = pl.pallas_call(
        first_kernel,
        out_shape=shape(K, 2 * K),
        in_specs=[SMEM] + [VMEM] * 3,
        out_specs=VMEM,
        compiler_params=LIMIT,
        cost_estimate=cost(3 * FIRST),
        name="first",
    )(meta, *extras)
    r, inv = pl.pallas_call(
        rest_kernel,
        out_shape=(shape(K, K), shape(2 * K, K, dtype=BF16)),
        in_specs=[VMEM],
        out_specs=(VMEM,) * 2,
        scratch_shapes=[pltpu.VMEM((K, 2 * K), F32)],
        compiler_params=LIMIT,
        cost_estimate=cost(12 - 3 * FIRST),
        name="rest",
    )(begun)
    q = pl.pallas_call(
        q_kernel,
        out_shape=shape(2 * HALF, K, dtype=BF16),
        in_specs=[VMEM] * 2,
        out_specs=VMEM,
        compiler_params=LIMIT,
        cost_estimate=cost(2),
        name="q",
    )(slab, inv)
    z = pl.pallas_call(
        solve_kernel,
        out_shape=shape(CB * TILE, K),
        in_specs=[SMEM] + [VMEM] * 5,
        out_specs=HBM,
        scratch_shapes=[pltpu.VMEM((4, 8 * ROWS, K), F32), pltpu.SemaphoreType.DMA((4,))],
        compiler_params=LIMIT,
        name="z",
    )(meta, *bodies, inv)
    return q, r, z


def solution(mesh):
    grid = Mesh(mesh.devices.reshape(8, 4, 4, 2), ("z", "x", "y", "c"))
    row, col = ("z", "x"), ("y", "c")
    placed = (
        P(row, col, None, None, None),
        P(row, col, None),
        P(row, col, None),
        P(row, col),
        P(col, None),
    )
    return jax.shard_map(
        on_device,
        mesh=grid,
        in_specs=placed,
        out_specs=(P(row, None), P(), P(col, None)),
        check_vma=False,
    )
```
